256 devices in a mesh: frame: 2 (over x_lo), tile: 128 (over z, y, x_hi, core).
Axes of the slice: x: 4 (x_hi: 2, x_lo: 2; x = x_hi * 2 + x_lo), y: 4, z: 8, core: 2. Of those that a mesh axis runs over, the one named last changes fastest.
Arguments:
- tokens: bfloat16 [4, 24576, 1024], P('frame', 'tile'), may hold values from -6 to 6
- norm_gain: float32 [1024], replicated, may hold values from 0.1 to 1.9
- modulation: float32 [4, 1024], P('frame'), may hold values from -1.5 to 6
- w_query: bfloat16 [1024, 1024], replicated, may hold values from -0.1875 to 0.1875
- w_key: bfloat16 [1024, 1024], replicated, may hold values from -0.1875 to 0.1875
- w_value: bfloat16 [1024, 1024], replicated, may hold values from -0.1875 to 0.1875
- w_out: bfloat16 [1024, 1024], replicated, may hold values from -0.1875 to 0.1875
- neigh_list: int32 [128, 3, 6], P('tile'), may hold values from 0 to 8
- neigh_count: int32 [128, 3], P('tile'), may hold values from 1 to 6, as said below
- cross_list: int32 [4, 128, 3, 4], P('frame', 'tile'), may hold values from 0 to 11
Outputs:
- update: bfloat16 [4, 24576, 1024], P('frame', 'tile')
The draws below stay inside these ranges and needn't reach their ends.
Inputs may be any that keep to these rules, and one draw needn't show every extreme that they name: `neigh_list`: an entry names a block of the extended row of tiles west, own and east, in that order. `neigh_count`: some query block uses all 6 slots. `cross_list`: an entry is frame * 3 + block at the query's own tile.
All inputs are finite; a program needn't handle non-finite values.
Results may differ from the reference program's by a relative error of at most 0.006.
The reference program's roundings to bfloat16 on the way (of `normed`, `weights` and `attended`) count: a program that leaves them out, or rounds other values in their place, can miss the bound.
Values may be sent and summed in bfloat16 or wider, within the bound.
No kernel may reach another device: no remote copies, remote signals or barrier semaphores. Data moves between devices by JAX's collectives and lax.ppermute only.
A program may use at most 128 MiB of HBM per device.

```python
import jax
import jax.numpy as jnp
from jax import lax

D = 1024
HEADS = 16
FRAMES = 4
BT = 64
NBLK = 3
NS = 6
CS = 4
TILES = 128
TILE_TOK = 192


def draw_neigh_count(key, part):
    key = jax.random.fold_in(key, 11)
    counts = jax.random.randint(key, (TILES, NBLK), 1, NS + 1)
    return counts.at[0, 0].set(NS).astype(jnp.int32)


def draw_modulation(key, part):
    key = jax.random.fold_in(key, 23)
    values = jnp.clip(0.3 * jax.random.normal(key, (FRAMES, D), jnp.float32), -1.5, 1.5)
    return values.astype(jnp.float32)


def plant(entries, rng, low, largest):
    longest = entries.shape.index(max(entries.shape))
    spots = []
    for shift in (0, 1):
        where = [jax.random.randint(jax.random.fold_in(rng, axis), (), 0, length) for axis, length in enumerate(entries.shape)]
        where[longest] = (where[longest] + shift) % entries.shape[longest]
        spots.append(tuple(where))
    return entries.at[spots[0]].set(low).at[spots[1]].set(largest)


def block_scale(stream_key, dims, split, least, high):
    def one(position, shards_of):
        steps = jax.random.uniform(jax.random.fold_in(jax.random.fold_in(stream_key, 6), position), (shards_of,), jnp.float32, least / len(split), high / len(split))
        return jnp.repeat(jnp.exp(steps), dims[position] // shards_of).reshape((-1,) + (1,) * (len(dims) - position - 1))

    level = one(*split[0])
    for cut in split[1:]:
        level = level * one(*cut)
    return level


def scatter_about(own_key, shape, width, reach, split=(), kind=jnp.bfloat16):
    values = width * jax.random.normal(own_key, shape, jnp.float32)
    if split:
        values = values * block_scale(own_key, shape, split, -0.22, 0.18)
    return jnp.clip(values, -reach, reach).astype(kind)


def setup_inputs(seed: int = 0) -> dict:
    keys = jax.random.split(jax.random.key(seed), 11)
    return {
        "tokens": scatter_about(keys[0], (FRAMES, TILES * TILE_TOK, D), 1.0, 6.0, ((0, 2), (1, 128))),
        "norm_gain": jnp.clip(1.0 + 0.18 * jax.random.normal(keys[1], (D,), jnp.float32), 0.1, 1.9),
        "modulation": draw_modulation(jax.random.fold_in(keys[10], 71), 0),
        "w_query": scatter_about(keys[3], (D, D), D ** -0.5, 0.1875),
        "w_key": scatter_about(keys[4], (D, D), D ** -0.5, 0.1875),
        "w_value": scatter_about(keys[5], (D, D), D ** -0.5, 0.1875),
        "w_out": scatter_about(keys[6], (D, D), D ** -0.5, 0.1875),
        "neigh_list": plant(jax.random.randint(keys[7], (TILES, NBLK, NS), 0, 3 * NBLK), jax.random.fold_in(keys[7], 1), 0, (3 * NBLK) - 1).astype(jnp.int32),
        "neigh_count": draw_neigh_count(jax.random.fold_in(keys[10], 71), 0),
        "cross_list": plant(jax.random.randint(keys[9], (FRAMES, TILES, NBLK, CS), 0, FRAMES * NBLK), jax.random.fold_in(keys[9], 1), 0, (FRAMES * NBLK) - 1).astype(jnp.int32),
    }


def normalize(tokens, norm_gain, modulation):
    values32 = tokens.astype(jnp.float32)
    meansq = lax.optimization_barrier(jnp.mean(values32 * values32, axis=-1, keepdims=True))
    scaled = values32 * lax.rsqrt(meansq + 1e-06) * norm_gain * (1.0 + modulation[:, None, :])
    return scaled.astype(jnp.bfloat16)

def attend(queries, near_k, near_v, far_k, far_v, near_list, near_count, far_list):
    frames_here, blocks, block_tok, model_width = queries.shape
    ext_blocks = near_k.shape[1]
    head_size = model_width // HEADS
    offset = (jnp.arange(frames_here, dtype=jnp.int32) * ext_blocks)[:, None, None]
    near_index = (offset + near_list[None]).astype(jnp.int32)
    flat_k = near_k.reshape(frames_here * ext_blocks, block_tok, model_width)
    flat_v = near_v.reshape(frames_here * ext_blocks, block_tok, model_width)
    key_set = jnp.concatenate([flat_k[near_index], far_k[far_list]], axis=2)
    value_set = jnp.concatenate([flat_v[near_index], far_v[far_list]], axis=2)
    slot_count = key_set.shape[2]
    key_set = key_set.reshape(frames_here, blocks, slot_count * block_tok, HEADS, head_size)
    value_set = value_set.reshape(frames_here, blocks, slot_count * block_tok, HEADS, head_size)
    usable = jnp.concatenate([jnp.arange(NS, dtype=jnp.int32)[None, :] < near_count[:, None], jnp.ones((blocks, far_list.shape[-1]), bool)], axis=1)
    usable = jnp.repeat(usable, block_tok, axis=1)
    mask_bias = jnp.where(usable, jnp.float32(0.0), jnp.float32(-1e+30))
    heads_q = queries.reshape(frames_here, blocks, block_tok, HEADS, head_size)
    scores = jnp.einsum('fbqhd,fbkhd->fbhqk', heads_q.astype(jnp.float32), key_set.astype(jnp.float32)) / jnp.sqrt(jnp.float32(head_size))
    scores = scores + mask_bias[None, :, None, None, :]
    peak_score = lax.optimization_barrier(jnp.max(scores, axis=-1, keepdims=True))
    shifted = jnp.exp(scores - peak_score)
    weights = (shifted / lax.optimization_barrier(jnp.sum(shifted, axis=-1, keepdims=True))).astype(jnp.bfloat16)
    attended = jnp.einsum('fbhqk,fbkhd->fbqhd', weights.astype(jnp.float32), value_set.astype(jnp.float32))
    return attended.astype(jnp.bfloat16).reshape(frames_here, blocks, block_tok, model_width)

def project(rows, weight):
    return jnp.dot(rows, weight, preferred_element_type=jnp.float32).astype(jnp.bfloat16)

def reference(tokens, norm_gain, modulation, w_query, w_key, w_value, w_out, neigh_list, neigh_count, cross_list):
    normed = normalize(tokens, norm_gain, modulation)
    flat_rows = normed.reshape(-1, D)
    shape5 = (FRAMES, TILES, NBLK, BT, D)
    queries = project(flat_rows, w_query).reshape(shape5)
    keys_all = project(flat_rows, w_key).reshape(shape5)
    values_all = project(flat_rows, w_value).reshape(shape5)

    def one_tile(tile_index):
        west = (tile_index - 1 + TILES) % TILES
        east = (tile_index + 1) % TILES
        near_k = jnp.concatenate([keys_all[:, west], keys_all[:, tile_index], keys_all[:, east]], axis=1)
        near_v = jnp.concatenate([values_all[:, west], values_all[:, tile_index], values_all[:, east]], axis=1)
        far_k = keys_all[:, tile_index].reshape(FRAMES * NBLK, BT, D)
        far_v = values_all[:, tile_index].reshape(FRAMES * NBLK, BT, D)
        return attend(queries[:, tile_index], near_k, near_v, far_k, far_v, neigh_list[tile_index], neigh_count[tile_index], cross_list[:, tile_index])
    attended = lax.map(one_tile, jnp.arange(TILES, dtype=jnp.int32))
    attended = jnp.transpose(attended, (1, 0, 2, 3, 4)).reshape(-1, D)
    update = jnp.dot(attended, w_out, preferred_element_type=jnp.float32).astype(jnp.bfloat16)
    return update.reshape(FRAMES, TILES * TILE_TOK, D)
```

```python
import functools

import jax
import jax.numpy as jnp
import numpy as np
from jax import lax
from jax.experimental import pallas as pl
from jax.experimental.pallas import tpu as pltpu
from jax.sharding import PartitionSpec as P

HEADS = 16
NS = 6
CS = 4
SLOTS = NS + CS
BT = 64
NBLK = 3
D = 1024
HEAD = D // HEADS
GROUP = 4
GW = GROUP * HEAD
TOK = NBLK * BT
ROWS = 2 * TOK
CHUNKS = 4
CR = ROWS // CHUNKS
BOTH = ("frame", "tile")
VMEM = pl.BlockSpec(memory_space=pltpu.VMEM)
SMEM = pl.BlockSpec(memory_space=pltpu.SMEM)
ANY = pl.BlockSpec(memory_space=pl.ANY)
EXP_SCALE = float(np.log2(np.e) / np.sqrt(HEAD))


def params(limit):
    return pltpu.CompilerParams(vmem_limit_bytes=limit)


def cost(flops, nbytes):
    return pl.CostEstimate(flops=int(flops), bytes_accessed=int(nbytes), transcendentals=0)


def norm_kernel(tok_ref, gain_ref, mod_ref, whole_ref, *chunk_refs):
    for i in range(CHUNKS):
        frame, row = divmod(i * CR, TOK)
        x = tok_ref[frame, row : row + CR, :].astype(jnp.float32)
        meansq = jnp.mean(x * x, axis=-1, keepdims=True)
        scaled = x * lax.rsqrt(meansq + 1e-06) * gain_ref[...] * (1.0 + mod_ref[frame : frame + 1, :])
        normed = scaled.astype(jnp.bfloat16)
        whole_ref[i * CR : (i + 1) * CR, :] = normed
        chunk_refs[i][...] = normed


def norm(tokens, gain, mod):
    chunk = jax.ShapeDtypeStruct((CR, D), jnp.bfloat16)
    return pl.pallas_call(
        norm_kernel,
        out_shape=[jax.ShapeDtypeStruct((ROWS, D), jnp.bfloat16)] + [chunk] * CHUNKS,
        in_specs=[VMEM] * 3,
        out_specs=[VMEM] * (1 + CHUNKS),
        compiler_params=params(8 << 20),
        cost_estimate=cost(ROWS * D * 8, ROWS * D * 6),
    )(tokens, gain, mod)


def project_into(x_ref, w_ref, out_ref, at):
    rows = x_ref.shape[0]
    for c in range(0, D, 256):
        out_ref[at : at + rows, c : c + 256] = jnp.dot(
            x_ref[...], w_ref[:, c : c + 256], preferred_element_type=jnp.float32
        ).astype(jnp.bfloat16)


def own_kernel(x_ref, wq_ref, wk_ref, wv_ref, q_ref, k_ref, v_ref):
    project_into(x_ref, wq_ref, q_ref, 0)
    project_into(x_ref, wk_ref, k_ref, 0)
    project_into(x_ref, wv_ref, v_ref, 0)


def own_project(x, wq, wk, wv):
    held = jax.ShapeDtypeStruct((4 * ROWS, D), jnp.bfloat16)
    return pl.pallas_call(
        own_kernel,
        out_shape=[jax.ShapeDtypeStruct((ROWS, D), jnp.bfloat16), held, held],
        in_specs=[VMEM] * 4,
        out_specs=[VMEM] * 3,
        compiler_params=params(8 << 20),
        cost_estimate=cost(6 * ROWS * D * D, 8 * D * D),
    )(x, wq, wk, wv)


def kv_kernel(ats, *refs):
    n = len(ats)
    wk_ref, wv_ref, _, _, k_ref, v_ref = refs[n:]
    for x_ref, at in zip(refs[:n], ats):
        project_into(x_ref, wk_ref, k_ref, at)
        project_into(x_ref, wv_ref, v_ref, at)


def kv_project(xs, ats, wk, wv, keys, values):
    n = len(xs)
    rows = sum(x.shape[0] for x in xs)
    held = jax.ShapeDtypeStruct((4 * ROWS, D), jnp.bfloat16)
    return pl.pallas_call(
        functools.partial(kv_kernel, ats),
        out_shape=[held, held],
        in_specs=[VMEM] * (n + 4),
        out_specs=[VMEM] * 2,
        input_output_aliases={n + 2: 0, n + 3: 1},
        compiler_params=params(8 << 20),
        cost_estimate=cost(4 * rows * D * D, 6 * D * D),
    )(*xs, wk, wv, keys, values)


def attend_kernel(frame, slot_ref, count_ref, q_ref, k_ref, v_ref, wo_ref, *rest):
    out_ref, att_ref, upd_ref, sem = rest[-4:]
    r = lax.broadcasted_iota(jnp.int32, (GW, GW), 0) // HEAD
    c = lax.broadcasted_iota(jnp.int32, (GW, GW), 1) // HEAD
    diagonal = r == c
    lane = lax.broadcasted_iota(jnp.int32, (1, SLOTS * BT), 1) // BT

    def block(b, g):
        u = frame * NBLK + b
        cols = slice(g * GW, (g + 1) * GW)
        q = q_ref[u * BT : (u + 1) * BT, cols]
        q4 = jnp.concatenate([q] * GROUP, axis=0)
        q4 = jnp.where(diagonal, q4, jnp.zeros_like(q4))
        at = [pl.ds(pl.multiple_of(slot_ref[u * SLOTS + s] * BT, BT), BT) for s in range(SLOTS)]
        keys = jnp.concatenate([k_ref[a, cols] for a in at], axis=0)
        values = jnp.concatenate([v_ref[a, cols] for a in at], axis=0)
        scores = lax.dot_general(
            q4, keys, (((1,), (1,)), ((), ())), preferred_element_type=jnp.float32
        )
        unused = (lane >= count_ref[b]) & (lane < NS)
        scores = scores + jnp.where(unused, jnp.float32(-1e30), jnp.float32(0.0))
        peak = jnp.max(scores, axis=1, keepdims=True)
        weights = jnp.exp2((scores - peak) * EXP_SCALE)
        total = jnp.sum(weights, axis=1, keepdims=True)
        att = jnp.dot(weights.astype(jnp.bfloat16), values, preferred_element_type=jnp.float32)
        att = jnp.where(diagonal, att * (1.0 / total), 0.0)
        att = sum(att[h * BT : (h + 1) * BT] for h in range(GROUP))
        att_ref[b * BT : (b + 1) * BT, cols] = att.astype(jnp.bfloat16)

    for g in range(D // GW):
        for b in range(NBLK):
            block(b, g)
    copies = []
    for i, col in enumerate(range(0, D, 256)):
        upd_ref[:, col : col + 256] = jnp.dot(
            att_ref[...], wo_ref[:, col : col + 256], preferred_element_type=jnp.float32
        ).astype(jnp.bfloat16)
    copy = pltpu.make_async_copy(upd_ref, out_ref.at[frame], sem)
    copy.start()
    copy.wait()


def attend(frame, slots, counts, queries, keys, values, w_out, earlier=None):
    extra = [] if earlier is None else [earlier]
    return pl.pallas_call(
        functools.partial(attend_kernel, frame),
        out_shape=jax.ShapeDtypeStruct((2, TOK, D), jnp.bfloat16),
        in_specs=[SMEM] * 2 + [VMEM] * 4 + [ANY] * len(extra),
        out_specs=ANY,
        scratch_shapes=[
            pltpu.VMEM((TOK, D), jnp.bfloat16),
            pltpu.VMEM((TOK, D), jnp.bfloat16),
            pltpu.SemaphoreType.DMA,
        ],
        input_output_aliases={6: 0} if extra else {},
        compiler_params=params(16 << 20),
        cost_estimate=cost(2 * TOK * D * D + 16 * TOK * SLOTS * BT * D, 8 * D * D),
    )(slots, counts, queries, keys, values, w_out, *extra)


def slot_table(neigh, cross, parity, mine):
    side = neigh // NBLK
    source = jnp.where(side == 1, 0, jnp.where((side == 2) == (parity == 0), 2, 3))
    near = source * 2 * NBLK + neigh % NBLK
    near = near[None] + NBLK * jnp.arange(2, dtype=jnp.int32)[:, None, None]
    owner = cross // (2 * NBLK)
    far = jnp.where(owner == mine, 0, 2 * NBLK) + cross % (2 * NBLK)
    return jnp.concatenate([near, far], axis=-1).reshape(-1)


def local(tokens, norm_gain, modulation, w_query, w_key, w_value, w_out, neigh_list, neigh_count, cross_list):
    tiles = lax.axis_size("tile")
    mine = lax.axis_index("frame")
    tile = lax.axis_index("tile")

    def device(f, t):
        return f * tiles + t % tiles

    cells = [(f, t) for f in range(2) for t in range(tiles)]
    partner = [(device(f, t), device(1 - f, t)) for f, t in cells]
    pair = [(device(f, t), device(f, t ^ 1)) for f, t in cells]
    onward = [(device(f, t), device(1 - f, t + 1 if t % 2 else t - 1)) for f, t in cells]

    slots = slot_table(neigh_list[0], cross_list[:, 0], tile % 2, mine)
    whole, *chunks = norm(tokens, norm_gain[None], modulation)
    swapped = [lax.ppermute(c, BOTH, partner) for c in chunks]
    across = lax.ppermute(whole, BOTH, pair)
    beyond = [lax.ppermute(s, BOTH, onward) for s in swapped]

    queries, keys, values = own_project(whole, w_query, w_key, w_value)
    keys, values = kv_project([across], [2 * ROWS], w_key, w_value, keys, values)
    for i in range(CHUNKS):
        keys, values = kv_project([swapped[i]], [ROWS + i * CR], w_key, w_value, keys, values)
        if i:
            keys, values = kv_project([beyond[i - 1]], [3 * ROWS + (i - 1) * CR], w_key, w_value, keys, values)
    last = CHUNKS - 1
    first = attend(0, slots, neigh_count[0], queries, keys, values, w_out)
    keys, values = kv_project([beyond[last]], [3 * ROWS + last * CR], w_key, w_value, keys, values)
    return attend(1, slots, neigh_count[0], queries, keys, values, w_out, first)


def solution(mesh):
    return jax.shard_map(
        local,
        mesh=mesh,
        in_specs=(
            P("frame", "tile", None),
            P(),
            P("frame", None),
            P(),
            P(),
            P(),
            P(),
            P("tile", None, None),
            P("tile", None),
            P("frame", "tile", None, None),
        ),
        out_specs=P("frame", "tile", None),
        check_vma=False,
    )
```

```python
import functools
import math

import jax
import jax.numpy as jnp
import numpy as np
from jax import lax
from jax.experimental import pallas as pl
from jax.experimental.pallas import tpu as pltpu
from jax.sharding import PartitionSpec as P

HEADS = 16
NS = 6
CS = 4
SLOTS = NS + CS
BT = 64
NBLK = 3
D = 1024
HEAD = D // HEADS
GROUP = 4
GW = GROUP * HEAD
TOK = NBLK * BT
ROWS = 2 * TOK
CHUNKS = 3
CR = ROWS // CHUNKS
STEP = math.gcd(CR, TOK)
BOTH = ("frame", "tile")
VMEM = pl.BlockSpec(memory_space=pltpu.VMEM)
ANY = pl.BlockSpec(memory_space=pl.ANY)
EXP_SCALE = float(np.log2(np.e) / np.sqrt(HEAD))


def params(limit):
    return pltpu.CompilerParams(vmem_limit_bytes=limit)


def in_hbm(x):
    return pltpu.with_memory_space_constraint(x, pltpu.HBM)


def cost(flops, nbytes):
    return pl.CostEstimate(flops=int(flops), bytes_accessed=int(nbytes), transcendentals=0)


def norm_kernel(tok_hbm, gain_hbm, mod_hbm, whole_ref, *rest):
    chunk_refs, (tok_ref, gain_ref, mod_ref, sems) = rest[:CHUNKS], rest[CHUNKS:]
    side = [
        pltpu.make_async_copy(gain_hbm, gain_ref, sems.at[ROWS // STEP]),
        pltpu.make_async_copy(mod_hbm, mod_ref, sems.at[ROWS // STEP + 1]),
    ]
    loads = []
    for i in range(ROWS // STEP):
        frame, row = divmod(i * STEP, TOK)
        rows = pl.ds(row, STEP)
        loads.append(
            pltpu.make_async_copy(tok_hbm.at[frame, rows], tok_ref.at[frame, rows], sems.at[i])
        )
    for copy in loads[:1] + side + loads[1:]:
        copy.start()
    for copy in side:
        copy.wait()
    for i in range(ROWS // STEP):
        frame, row = divmod(i * STEP, TOK)
        loads[i].wait()
        x = tok_ref[frame, row : row + STEP, :].astype(jnp.float32)
        meansq = jnp.mean(x * x, axis=-1, keepdims=True)
        scaled = x * lax.rsqrt(meansq + 1e-06) * gain_ref[...] * (1.0 + mod_ref[frame : frame + 1, :])
        normed = scaled.astype(jnp.bfloat16)
        whole_ref[i * STEP : (i + 1) * STEP, :] = normed
        chunk, row = divmod(i * STEP, CR)
        chunk_refs[chunk][row : row + STEP, :] = normed


def norm(tokens, gain, mod):
    chunk = jax.ShapeDtypeStruct((CR, D), jnp.bfloat16)
    return pl.pallas_call(
        norm_kernel,
        out_shape=[jax.ShapeDtypeStruct((ROWS, D), jnp.bfloat16)] + [chunk] * CHUNKS,
        in_specs=[ANY] * 3,
        out_specs=[VMEM] * (1 + CHUNKS),
        scratch_shapes=[
            pltpu.VMEM((2, TOK, D), jnp.bfloat16),
            pltpu.VMEM((1, D), jnp.float32),
            pltpu.VMEM((2, D), jnp.float32),
            pltpu.SemaphoreType.DMA((ROWS // STEP + 2,)),
        ],
        compiler_params=params(8 << 20),
        cost_estimate=cost(ROWS * D * 8, ROWS * D * 6),
    )(*map(in_hbm, (tokens, gain, mod)))


def project_into(x, w_ref, out_ref, at, width=256):
    rows = x.shape[0]
    for c in range(0, D, width):
        out_ref[at : at + rows, c : c + width] = jnp.dot(
            x, w_ref[:, c : c + width], preferred_element_type=jnp.float32
        ).astype(jnp.bfloat16)


def own_kernel(x_ref, wk_hbm, wv_hbm, wq_hbm, *refs):
    k_ref, v_ref, q_ref, wk_ref, wv_ref, wq_ref, sems = refs[-7:]
    steps = ((wq_hbm, wq_ref, q_ref), (wk_hbm, wk_ref, k_ref), (wv_hbm, wv_ref, v_ref))
    loads = [
        pltpu.make_async_copy(hbm, vmem, sems.at[i]) for i, (hbm, vmem, _) in enumerate(steps)
    ]
    for copy in loads[:2]:
        copy.start()
    for i, (_, w_ref, out_ref) in enumerate(steps):
        loads[i].wait()
        if i + 2 < len(loads):
            loads[i + 2].start()
        project_into(x_ref[...], w_ref, out_ref, 0)


def own_project(x, wq, wk, wv, later):
    n = len(later)
    rows = pltpu.VMEM((ROWS, D), jnp.bfloat16)
    weight = pltpu.VMEM((D, D), jnp.bfloat16)
    return pl.pallas_call(
        own_kernel,
        out_shape=[jax.ShapeDtypeStruct(c.shape, c.dtype) for c in later] + [rows] * 3 + [weight] * 2,
        in_specs=[VMEM] + [ANY] * 3 + [VMEM] * n,
        out_specs=[VMEM] * (n + 5),
        input_output_aliases={4 + i: i for i in range(n)},
        scratch_shapes=[pltpu.VMEM((D, D), jnp.bfloat16), pltpu.SemaphoreType.DMA((3,))],
        compiler_params=params(12 << 20),
        cost_estimate=cost(6 * ROWS * D * D, 6 * D * D),
    )(x, *map(in_hbm, (wk, wv, wq)), *later)


def gate_kernel(*refs):
    pass


def gate(x, after):
    return pl.pallas_call(
        gate_kernel,
        out_shape=jax.ShapeDtypeStruct(x.shape, x.dtype),
        in_specs=[VMEM] * 2,
        out_specs=VMEM,
        input_output_aliases={0: 0},
        compiler_params=params(1 << 20),
    )(x, after)


def kv_kernel(ats, n_copies, *refs):
    n = len(ats)
    wk_ref, wv_ref = refs[n : n + 2]
    sources = refs[n + 2 : n + 2 + len(n_copies)]
    k_ref, v_ref, token_ref = refs[-4:-1] if n_copies else refs[-3:]
    token_ref[...] = jnp.zeros_like(token_ref)
    copies = []
    for source, (side, at) in zip(sources, n_copies):
        target = (k_ref, v_ref)[side].at[pl.ds(at, ROWS)]
        copies.append(pltpu.make_async_copy(source, target, refs[-1].at[len(copies)]))
        copies[-1].start()
    x = jnp.concatenate([ref[...] for ref in refs[:n]], axis=0) if n > 1 else refs[0][...]
    for w_ref, out_ref in ((wk_ref, k_ref), (wv_ref, v_ref)):
        for c in range(0, D, 256):
            y = jnp.dot(x, w_ref[:, c : c + 256], preferred_element_type=jnp.float32).astype(jnp.bfloat16)
            row = 0
            for ref, at in zip(refs[:n], ats):
                rows = ref.shape[0]
                out_ref[at : at + rows, c : c + 256] = y[row : row + rows]
                row += rows
    for copy in copies:
        copy.wait()


def kv_project(xs, ats, wk, wv, held=None, copied=()):
    n, m = len(xs), len(copied)
    rows = sum(x.shape[0] for x in xs)
    shape = pltpu.VMEM((4 * ROWS, D), jnp.bfloat16)
    extra = [] if held is None else list(held)
    return pl.pallas_call(
        functools.partial(kv_kernel, ats, [c[1:] for c in copied]),
        out_shape=[shape, shape, jax.ShapeDtypeStruct((8, 128), jnp.float32)],
        in_specs=[VMEM] * (n + 2 + m + len(extra)),
        out_specs=[VMEM] * 3,
        input_output_aliases={n + 2 + m: 0, n + 3 + m: 1} if extra else {},
        scratch_shapes=[pltpu.SemaphoreType.DMA((m,))] if m else [],
        compiler_params=params(8 << 20),
        cost_estimate=cost(4 * rows * D * D, 6 * D * D),
    )(*xs, wk, wv, *[c[0] for c in copied], *extra)


def attend_kernel(frame, *refs):
    neigh_hbm, count_hbm, cross_hbm, q_ref, k_ref, v_ref, wo_hbm = refs[:7]
    out_ref, wo_ref, att_ref, upd_ref, neigh_ref, count_ref, cross_ref, sems = refs[-8:]
    lists = [
        pltpu.make_async_copy(neigh_hbm, neigh_ref, sems.at[0]),
        pltpu.make_async_copy(count_hbm, count_ref, sems.at[1]),
        pltpu.make_async_copy(cross_hbm, cross_ref, sems.at[2]),
    ]
    wo_copy = pltpu.make_async_copy(wo_hbm, wo_ref, sems.at[4])
    for copy in lists + [wo_copy]:
        copy.start()
    for copy in lists:
        copy.wait()
    mine = lax.axis_index("frame")
    odd = lax.axis_index("tile") % 2
    r = lax.broadcasted_iota(jnp.int32, (GW, GW), 0) // HEAD
    c = lax.broadcasted_iota(jnp.int32, (GW, GW), 1) // HEAD
    diagonal = r == c
    lane = lax.broadcasted_iota(jnp.int32, (1, SLOTS * BT), 1) // BT

    def rows_of(block):
        return pl.ds(pl.multiple_of(block * BT, BT), BT)

    def slots(b):
        found = []
        for s in range(NS):
            e = neigh_ref[0, b, s]
            side = e // NBLK
            core = jnp.where(side == 2, odd == 0, odd == 1)
            source = jnp.where(side == 1, 0, jnp.where(core, 2, 3))
            found.append(source * (2 * NBLK) + frame * NBLK + (e - side * NBLK))
        for s in range(CS):
            e = cross_ref[frame, 0, b, s]
            owner = e // (2 * NBLK)
            found.append(e - owner * (2 * NBLK) + jnp.where(owner == mine, 0, 2 * NBLK))
        return [rows_of(f) for f in found]

    def block(b, g, at):
        u = frame * NBLK + b
        cols = slice(g * GW, (g + 1) * GW)
        q = q_ref[u * BT : (u + 1) * BT, cols]
        q4 = jnp.concatenate([q] * GROUP, axis=0)
        q4 = jnp.where(diagonal, q4, jnp.zeros_like(q4))
        keys = jnp.concatenate([k_ref[a, cols] for a in at], axis=0)
        values = jnp.concatenate([v_ref[a, cols] for a in at], axis=0)
        scores = lax.dot_general(
            q4, keys, (((1,), (1,)), ((), ())), preferred_element_type=jnp.float32
        )
        unused = (lane >= count_ref[0, b]) & (lane < NS)
        scores = scores + jnp.where(unused, jnp.float32(-1e30), jnp.float32(0.0))
        peak = jnp.max(scores, axis=1, keepdims=True)
        weights = jnp.exp2((scores - peak) * EXP_SCALE)
        total = jnp.sum(weights, axis=1, keepdims=True)
        weights = (weights * (1.0 / total)).astype(jnp.bfloat16)
        att = jnp.dot(weights, values, preferred_element_type=jnp.float32)
        att = jnp.where(diagonal, att, 0.0)
        att = sum(att[h * BT : (h + 1) * BT] for h in range(GROUP))
        att_ref[b * BT : (b + 1) * BT, cols] = att.astype(jnp.bfloat16)

    at = [slots(b) for b in range(NBLK)]
    for g in range(D // GW):
        for b in range(NBLK):
            block(b, g, at[b])
    wo_copy.wait()
    project_into(att_ref[...], wo_ref, upd_ref, 0)
    copy = pltpu.make_async_copy(upd_ref, out_ref.at[frame], sems.at[3])
    copy.start()
    copy.wait()


def attend(frame, lists, queries, keys, values, w_out, earlier=None):
    extra = [] if earlier is None else [earlier]
    return pl.pallas_call(
        functools.partial(attend_kernel, frame),
        out_shape=jax.ShapeDtypeStruct((2, TOK, D), jnp.bfloat16),
        in_specs=[ANY] * 3 + [VMEM] * 3 + [ANY] * (1 + len(extra)),
        out_specs=ANY,
        scratch_shapes=[
            pltpu.VMEM((D, D), jnp.bfloat16),
            pltpu.VMEM((TOK, D), jnp.bfloat16),
            pltpu.VMEM((TOK, D), jnp.bfloat16),
        ]
        + [pltpu.SMEM(x.shape, jnp.int32) for x in lists]
        + [pltpu.SemaphoreType.DMA((5,))],
        input_output_aliases={7: 0} if extra else {},
        compiler_params=params(16 << 20),
        cost_estimate=cost(2 * TOK * D * D + 16 * TOK * SLOTS * BT * D, 8 * D * D),
    )(*lists, queries, keys, values, in_hbm(w_out), *extra)


def local(tokens, norm_gain, modulation, w_query, w_key, w_value, w_out, neigh_list, neigh_count, cross_list):
    tiles = lax.axis_size("tile")

    def device(f, t):
        return f * tiles + t % tiles

    cells = [(f, t) for f in range(2) for t in range(tiles)]
    partner = [(device(f, t), device(1 - f, t)) for f, t in cells]
    pair = [(device(f, t), device(f, t ^ 1)) for f, t in cells]
    onward = [(device(f, t), device(1 - f, t + 1 if t % 2 else t - 1)) for f, t in cells]

    def swap(x):
        return lax.ppermute(x, BOTH, partner)

    def cross(x):
        return lax.ppermute(x, BOTH, pair)

    def forward(x):
        return lax.ppermute(x, BOTH, onward)

    lists = (neigh_list, neigh_count, cross_list)
    whole, *chunks = norm(tokens, norm_gain[None], modulation)
    across = cross(whole)
    *later, own_k, own_v, queries, wk, wv = own_project(whole, w_query, w_key, w_value, chunks[2:])
    swapped = [swap(c) for c in chunks[:2] + later]

    def at(source, i):
        return source * ROWS + i * CR

    beyond, held = [], None
    for i, arrived in enumerate(swapped):
        if held is not None:
            arrived = gate(arrived, token)
        beyond.append(forward(arrived))
        if i == 0:
            *held, token = kv_project(
                [across, arrived], [2 * ROWS, at(1, 0)], wk, wv, None, [(own_k, 0, 0), (own_v, 1, 0)]
            )
        else:
            *held, token = kv_project([arrived, beyond[i - 1]], [at(1, i), at(3, i - 1)], wk, wv, held)
    first = attend(0, lists, queries, *held, w_out)
    *held, _ = kv_project([beyond[-1]], [at(3, CHUNKS - 1)], wk, wv, held)
    return attend(1, lists, queries, *held, w_out, first)


def solution(mesh):
    return jax.shard_map(
        local,
        mesh=mesh,
        in_specs=(
            P("frame", "tile", None),
            P(),
            P("frame", None),
            P(),
            P(),
            P(),
            P(),
            P("tile", None, None),
            P("tile", None),
            P("frame", "tile", None, None),
        ),
        out_specs=P("frame", "tile", None),
        check_vma=False,
    )
```

```python
import functools
import math

import jax
import jax.numpy as jnp
import numpy as np
from jax import lax
from jax.experimental import pallas as pl
from jax.experimental.pallas import tpu as pltpu
from jax.sharding import PartitionSpec as P

HEADS = 16
NS = 6
CS = 4
SLOTS = NS + CS
BT = 64
NBLK = 3
D = 1024
HEAD = D // HEADS
GROUP = 4
GW = GROUP * HEAD
TOK = NBLK * BT
ROWS = 2 * TOK
CHUNKS = 3
CR = ROWS // CHUNKS
STEP = math.gcd(CR, TOK)
BOTH = ("frame", "tile")
VMEM = pl.BlockSpec(memory_space=pltpu.VMEM)
ANY = pl.BlockSpec(memory_space=pl.ANY)
EXP_SCALE = float(np.log2(np.e) / np.sqrt(HEAD))


def params(limit):
    return pltpu.CompilerParams(vmem_limit_bytes=limit)


def in_hbm(x):
    return pltpu.with_memory_space_constraint(x, pltpu.HBM)


def cost(flops, nbytes):
    return pl.CostEstimate(flops=int(flops), bytes_accessed=int(nbytes), transcendentals=0)


def norm_kernel(tok_hbm, gain_hbm, mod_hbm, whole_ref, *rest):
    chunk_refs, (tok_ref, gain_ref, mod_ref, sems) = rest[:CHUNKS], rest[CHUNKS:]
    side = [
        pltpu.make_async_copy(gain_hbm, gain_ref, sems.at[ROWS // STEP]),
        pltpu.make_async_copy(mod_hbm, mod_ref, sems.at[ROWS // STEP + 1]),
    ]
    loads = []
    for i in range(ROWS // STEP):
        frame, row = divmod(i * STEP, TOK)
        rows = pl.ds(row, STEP)
        loads.append(
            pltpu.make_async_copy(tok_hbm.at[frame, rows], tok_ref.at[frame, rows], sems.at[i])
        )
    for copy in loads[:1] + side + loads[1:]:
        copy.start()
    for copy in side:
        copy.wait()
    for i in range(ROWS // STEP):
        frame, row = divmod(i * STEP, TOK)
        loads[i].wait()
        x = tok_ref[frame, row : row + STEP, :].astype(jnp.float32)
        meansq = jnp.mean(x * x, axis=-1, keepdims=True)
        scaled = x * lax.rsqrt(meansq + 1e-06) * gain_ref[...] * (1.0 + mod_ref[frame : frame + 1, :])
        normed = scaled.astype(jnp.bfloat16)
        whole_ref[i * STEP : (i + 1) * STEP, :] = normed
        chunk, row = divmod(i * STEP, CR)
        chunk_refs[chunk][row : row + STEP, :] = normed


def norm(tokens, gain, mod):
    chunk = jax.ShapeDtypeStruct((CR, D), jnp.bfloat16)
    return pl.pallas_call(
        norm_kernel,
        out_shape=[jax.ShapeDtypeStruct((ROWS, D), jnp.bfloat16)] + [chunk] * CHUNKS,
        in_specs=[ANY] * 3,
        out_specs=[VMEM] * (1 + CHUNKS),
        scratch_shapes=[
            pltpu.VMEM((2, TOK, D), jnp.bfloat16),
            pltpu.VMEM((1, D), jnp.float32),
            pltpu.VMEM((2, D), jnp.float32),
            pltpu.SemaphoreType.DMA((ROWS // STEP + 2,)),
        ],
        compiler_params=params(8 << 20),
        cost_estimate=cost(ROWS * D * 8, ROWS * D * 6),
    )(*map(in_hbm, (tokens, gain, mod)))


def project_into(x, w_ref, out_ref, at, width=256):
    rows = x.shape[0]
    for c in range(0, D, width):
        out_ref[at : at + rows, c : c + width] = jnp.dot(
            x, w_ref[:, c : c + width], preferred_element_type=jnp.float32
        ).astype(jnp.bfloat16)


def own_kernel(n, *refs):
    x_ref, hbms, refs = refs[0], refs[1:4], refs[4 + 2 * n :]
    out_refs, w_refs, sems = refs[:3], (refs[5], refs[3], refs[4]), refs[6]
    loads = [pltpu.make_async_copy(hbm, w, sems.at[i]) for i, (hbm, w) in enumerate(zip(hbms, w_refs))]
    for copy in loads[:2]:
        copy.start()
    for i, (w_ref, out_ref) in enumerate(zip(w_refs, out_refs)):
        loads[i].wait()
        if i + 2 < len(loads):
            loads[i + 2].start()
        project_into(x_ref[...], w_ref, out_ref, 0)


def own_project(x, weights, later=()):
    n = len(later)
    weight = pltpu.VMEM((D, D), jnp.bfloat16)
    out = pl.pallas_call(
        functools.partial(own_kernel, n),
        out_shape=[jax.ShapeDtypeStruct(c.shape, c.dtype) for c in later]
        + [pltpu.VMEM((ROWS, D), jnp.bfloat16)] * 3
        + [weight] * 2,
        in_specs=[VMEM] + [ANY] * 3 + [VMEM] * n,
        out_specs=[VMEM] * (n + 5),
        input_output_aliases={4 + i: i for i in range(n)},
        scratch_shapes=[weight, pltpu.SemaphoreType.DMA((3,))],
        compiler_params=params(12 << 20),
        cost_estimate=cost(6 * ROWS * D * D, 6 * D * D),
    )(x, *map(in_hbm, weights), *later)
    return out[:n], out[n : n + 3], out[n + 3 :]


def gate_kernel(*refs):
    pass


def gate(x, after):
    return pl.pallas_call(
        gate_kernel,
        out_shape=jax.ShapeDtypeStruct(x.shape, x.dtype),
        in_specs=[VMEM] * 2,
        out_specs=VMEM,
        input_output_aliases={0: 0},
        compiler_params=params(1 << 20),
    )(x, after)


def project_rows(x_refs, ats, pairs):
    x = jnp.concatenate([ref[...] for ref in x_refs], axis=0) if len(x_refs) > 1 else x_refs[0][...]
    for w_ref, out_ref in pairs:
        for c in range(0, D, 256):
            y = jnp.dot(x, w_ref[:, c : c + 256], preferred_element_type=jnp.float32).astype(jnp.bfloat16)
            row = 0
            for ref, at in zip(x_refs, ats):
                rows = ref.shape[0]
                out_ref[at : at + rows, c : c + 256] = y[row : row + rows]
                row += rows


def kv_kernel(ats, own, *refs):
    n = len(ats)
    wk_ref, wv_ref = refs[n : n + 2]
    k_ref, v_ref, token_ref = refs[n + 4 : n + 7]
    token_ref[...] = jnp.zeros_like(token_ref)
    copies = []
    if own:
        for i, (source, held_ref) in enumerate(zip(refs[n + 2 : n + 4], (k_ref, v_ref))):
            copies.append(pltpu.make_async_copy(source, held_ref.at[pl.ds(0, ROWS)], refs[-1].at[i]))
            copies[-1].start()
    project_rows(refs[:n], ats, ((wk_ref, k_ref), (wv_ref, v_ref)))
    for copy in copies:
        copy.wait()


def kv_project(xs, ats, wk, wv, held, own):
    n = len(xs)
    rows = sum(x.shape[0] for x in xs)
    shape = pltpu.VMEM((4 * ROWS, D), jnp.bfloat16)
    return pl.pallas_call(
        functools.partial(kv_kernel, ats, own),
        out_shape=[shape, shape, jax.ShapeDtypeStruct((8, 128), jnp.float32)],
        in_specs=[VMEM] * (n + 4),
        out_specs=[VMEM] * 3,
        input_output_aliases={} if own else {n + 2: 0, n + 3: 1},
        scratch_shapes=[pltpu.SemaphoreType.DMA((2,))] if own else [],
        compiler_params=params(8 << 20),
        cost_estimate=cost(4 * rows * D * D, 6 * D * D),
    )(*xs, wk, wv, *held)


def attend_kernel(ats, finish, *refs):
    refs = list(refs)

    def take(n):
        out = refs[:n]
        del refs[:n]
        return out

    x_refs = take(len(ats))
    wk_ref, wv_ref, q_ref, neigh_hbm, count_hbm, cross_hbm = take(6)
    take(2)
    if finish is not None:
        part_refs, (wo_hbm,) = take(3), take(1)
        take(finish)
    k_ref, v_ref = take(2)
    if finish is None:
        part_refs = take(3)
    else:
        (out_ref,) = take(1)
    neigh_ref, count_ref, cross_ref, sems = take(4)
    if finish is not None:
        wo_ref, att_ref, upd_ref = take(3)
    lists = [
        pltpu.make_async_copy(neigh_hbm, neigh_ref, sems.at[0]),
        pltpu.make_async_copy(count_hbm, count_ref, sems.at[1]),
        pltpu.make_async_copy(cross_hbm, cross_ref, sems.at[2]),
    ]
    for copy in lists:
        copy.start()
    if finish is not None:
        wo_copy = pltpu.make_async_copy(wo_hbm, wo_ref, sems.at[3])
        wo_copy.start()
    project_rows(x_refs, ats, ((wk_ref, k_ref), (wv_ref, v_ref)))
    for copy in lists:
        copy.wait()
    mine = lax.axis_index("frame")
    odd = lax.axis_index("tile") % 2
    r = lax.broadcasted_iota(jnp.int32, (GW, GW), 0) // HEAD
    c = lax.broadcasted_iota(jnp.int32, (GW, GW), 1) // HEAD
    diagonal = r == c
    even_head = lax.broadcasted_iota(jnp.int32, (BT, 2 * HEAD), 1) < HEAD
    lane = lax.broadcasted_iota(jnp.int32, (1, NS * BT), 1) // BT

    def rows_of(block):
        return pl.ds(pl.multiple_of(block * BT, BT), BT)

    def near_slots(frame, b):
        found = []
        for s in range(NS):
            e = neigh_ref[0, b, s]
            side = e // NBLK
            core = jnp.where(side == 2, odd == 0, odd == 1)
            source = jnp.where(side == 1, 0, jnp.where(core, 2, 3))
            found.append(rows_of(source * (2 * NBLK) + frame * NBLK + (e - side * NBLK)))
        return found

    def far_slots(frame, b):
        found = []
        for s in range(CS):
            e = cross_ref[frame, 0, b, s]
            owner = e // (2 * NBLK)
            found.append(rows_of(e - owner * (2 * NBLK) + jnp.where(owner == mine, 0, 2 * NBLK)))
        return found

    def own_columns(x):
        halves = []
        for h in range(0, GROUP, 2):
            two = slice(h * HEAD, (h + 2) * HEAD) if x.shape[1] > 1 else slice(0, 1)
            halves.append(
                jnp.where(even_head, x[h * BT : (h + 1) * BT, two], x[(h + 1) * BT : (h + 2) * BT, two])
            )
        return jnp.concatenate(halves, axis=1)

    def part(frame, b, g, at, masked):
        u = frame * NBLK + b
        cols = slice(g * GW, (g + 1) * GW)
        q = q_ref[u * BT : (u + 1) * BT, cols]
        q4 = jnp.concatenate([q] * GROUP, axis=0)
        q4 = jnp.where(diagonal, q4, jnp.zeros_like(q4))
        keys = jnp.concatenate([k_ref[a, cols] for a in at], axis=0)
        values = jnp.concatenate([v_ref[a, cols] for a in at], axis=0)
        scores = lax.dot_general(
            q4, keys, (((1,), (1,)), ((), ())), preferred_element_type=jnp.float32
        )
        if masked:
            scores = scores + jnp.where(lane < count_ref[0, b], jnp.float32(0.0), jnp.float32(-1e30))
        peak = jnp.max(scores, axis=1, keepdims=True)
        weights = jnp.exp2((scores - peak) * EXP_SCALE)
        total = jnp.sum(weights, axis=1, keepdims=True)
        att = jnp.dot(weights.astype(jnp.bfloat16), values, preferred_element_type=jnp.float32)
        return own_columns(att), own_columns(peak), own_columns(total)

    def parts(frame, slots, masked):
        at = [slots(frame, b) for b in range(NBLK)]
        for g in range(D // GW):
            for b in range(NBLK):
                where = (slice(b * BT, (b + 1) * BT), slice(g * GW, (g + 1) * GW))
                yield where, part(frame, b, g, at[b], masked)

    if finish is None:
        for frame in range(2):
            for where, values in parts(frame, far_slots, False):
                for ref, value in zip(part_refs, values):
                    ref[(frame, *where)] = value
        return
    for where, (att, peak, total) in parts(finish, near_slots, True):
        att2, peak2, total2 = (ref[(finish, *where)] for ref in part_refs)
        top = jnp.maximum(peak, peak2)
        scale, scale2 = jnp.exp2((peak - top) * EXP_SCALE), jnp.exp2((peak2 - top) * EXP_SCALE)
        whole = total * scale + total2 * scale2
        att_ref[where] = ((att * scale + att2 * scale2) / whole).astype(jnp.bfloat16)
    wo_copy.wait()
    copies = []
    for i, col in enumerate(range(0, D, 512)):
        cols = slice(col, col + 512)
        upd_ref[:, cols] = jnp.dot(
            att_ref[...], wo_ref[:, cols], preferred_element_type=jnp.float32
        ).astype(jnp.bfloat16)
        some = pl.ds(col, 512)
        copies.append(
            pltpu.make_async_copy(upd_ref.at[:, some], out_ref.at[finish, :, some], sems.at[4 + i])
        )
        copies[-1].start()
    for copy in copies:
        copy.wait()


def attend(xs, ats, wk, wv, held, queries, lists, finish=None, parts=(), w_out=None, earlier=()):
    n = len(xs)
    held_shape = pltpu.VMEM((4 * ROWS, D), jnp.bfloat16)
    args = [*xs, wk, wv, queries, *lists, *held]
    in_specs = [VMEM] * (n + 3) + [ANY] * 3 + [VMEM] * 2
    out_shape, out_specs = [held_shape] * 2, [VMEM] * 2
    aliases = {n + 6: 0, n + 7: 1}
    scratch = [pltpu.SMEM(x.shape, jnp.int32) for x in lists] + [pltpu.SemaphoreType.DMA((6,))]
    if finish is None:
        out_shape += [jax.ShapeDtypeStruct((2, TOK, D), jnp.float32)] * 3
        out_specs += [VMEM] * 3
    else:
        args += [*parts, in_hbm(w_out), *earlier]
        in_specs += [VMEM] * 3 + [ANY] * (1 + len(earlier))
        out_shape.append(jax.ShapeDtypeStruct((2, TOK, D), jnp.bfloat16))
        out_specs.append(ANY)
        if earlier:
            aliases[len(args) - 1] = 2
        scratch += [pltpu.VMEM((D, D), jnp.bfloat16)] + [pltpu.VMEM((TOK, D), jnp.bfloat16)] * 2
    return pl.pallas_call(
        functools.partial(attend_kernel, ats, finish),
        out_shape=out_shape,
        in_specs=in_specs,
        out_specs=out_specs,
        scratch_shapes=scratch,
        input_output_aliases=aliases,
        compiler_params=params(16 << 20),
        cost_estimate=cost(2 * TOK * D * D + 16 * TOK * SLOTS * BT * D, 8 * D * D),
    )(*args)


def local(tokens, norm_gain, modulation, w_query, w_key, w_value, w_out, neigh_list, neigh_count, cross_list):
    tiles = lax.axis_size("tile")

    def device(f, t):
        return f * tiles + t % tiles

    cells = [(f, t) for f in range(2) for t in range(tiles)]
    partner = [(device(f, t), device(1 - f, t)) for f, t in cells]
    pair = [(device(f, t), device(f, t ^ 1)) for f, t in cells]
    onward = [(device(f, t), device(1 - f, t + 1 if t % 2 else t - 1)) for f, t in cells]

    def swap(x):
        return lax.ppermute(x, BOTH, partner)

    def cross(x):
        return lax.ppermute(x, BOTH, pair)

    def forward(x):
        return lax.ppermute(x, BOTH, onward)

    def at(source, i):
        return source * ROWS + i * CR

    lists = (neigh_list, neigh_count, cross_list)
    whole, *chunks = norm(tokens, norm_gain[None], modulation)
    s0, s1 = swap(chunks[0]), swap(chunks[1])
    across = cross(whole)
    later, (queries, *own), (wk, wv) = own_project(whole, [w_query, w_key, w_value], [chunks[2]])
    s2 = swap(later[0])
    o0 = forward(s0)
    *held, token = kv_project([s0, across], [at(1, 0), 2 * ROWS], wk, wv, own, True)
    s1 = gate(s1, token)
    o1 = forward(s1)
    *held, token = kv_project([s1], [at(1, 1)], wk, wv, held, False)
    s2 = gate(s2, token)
    o2 = forward(s2)
    *held, att, peak, total = attend([s2], [at(1, 2)], wk, wv, held, queries, lists)
    parts = att, peak, total
    *held, first = attend([o0, o1], [at(3, 0), at(3, 1)], wk, wv, held, queries, lists, 0, parts, w_out)
    return attend([o2], [at(3, 2)], wk, wv, held, queries, lists, 1, parts, w_out, [first])[2]


def solution(mesh):
    return jax.shard_map(
        local,
        mesh=mesh,
        in_specs=(
            P("frame", "tile", None),
            P(),
            P("frame", None),
            P(),
            P(),
            P(),
            P(),
            P("tile", None, None),
            P("tile", None),
            P("frame", "tile", None, None),
        ),
        out_specs=P("frame", "tile", None),
        check_vma=False,
    )
```

```python
import functools
import math

import jax
import jax.numpy as jnp
import numpy as np
from jax import lax
from jax.experimental import pallas as pl
from jax.experimental.pallas import tpu as pltpu
from jax.sharding import PartitionSpec as P

HEADS = 16
NS = 6
CS = 4
SLOTS = NS + CS
BT = 64
NBLK = 3
D = 1024
HEAD = D // HEADS
GROUP = 4
GW = GROUP * HEAD
TOK = NBLK * BT
ROWS = 2 * TOK
CHUNKS = 3
CR = ROWS // CHUNKS
STEP = math.gcd(CR, TOK)
BOTH = ("frame", "tile")
VMEM = pl.BlockSpec(memory_space=pltpu.VMEM)
ANY = pl.BlockSpec(memory_space=pl.ANY)
FAR_AHEAD = 64.0
EXP_SCALE = float(np.log2(np.e) / np.sqrt(HEAD))


def params(limit):
    return pltpu.CompilerParams(vmem_limit_bytes=limit)


def in_hbm(x):
    return pltpu.with_memory_space_constraint(x, pltpu.HBM)


def cost(flops, nbytes):
    return pl.CostEstimate(flops=int(flops), bytes_accessed=int(nbytes), transcendentals=0)


def norm_kernel(tok_hbm, gain_hbm, mod_hbm, whole_ref, *rest):
    chunk_refs, (tok_ref, gain_ref, mod_ref, sems) = rest[:CHUNKS], rest[CHUNKS:]
    side = [
        pltpu.make_async_copy(gain_hbm, gain_ref, sems.at[ROWS // STEP]),
        pltpu.make_async_copy(mod_hbm, mod_ref, sems.at[ROWS // STEP + 1]),
    ]
    loads = []
    for i in range(ROWS // STEP):
        frame, row = divmod(i * STEP, TOK)
        rows = pl.ds(row, STEP)
        loads.append(
            pltpu.make_async_copy(tok_hbm.at[frame, rows], tok_ref.at[frame, rows], sems.at[i])
        )
    for copy in loads[:1] + side + loads[1:]:
        copy.start()
    for copy in side:
        copy.wait()
    for i in range(ROWS // STEP):
        frame, row = divmod(i * STEP, TOK)
        loads[i].wait()
        x = tok_ref[frame, row : row + STEP, :].astype(jnp.float32)
        meansq = jnp.mean(x * x, axis=-1, keepdims=True)
        scaled = x * lax.rsqrt(meansq + 1e-06) * gain_ref[...] * (1.0 + mod_ref[frame : frame + 1, :])
        normed = scaled.astype(jnp.bfloat16)
        whole_ref[i * STEP : (i + 1) * STEP, :] = normed
        chunk, row = divmod(i * STEP, CR)
        chunk_refs[chunk][row : row + STEP, :] = normed


def norm(tokens, gain, mod):
    chunk = jax.ShapeDtypeStruct((CR, D), jnp.bfloat16)
    return pl.pallas_call(
        norm_kernel,
        out_shape=[jax.ShapeDtypeStruct((ROWS, D), jnp.bfloat16)] + [chunk] * CHUNKS,
        in_specs=[ANY] * 3,
        out_specs=[VMEM] * (1 + CHUNKS),
        scratch_shapes=[
            pltpu.VMEM((2, TOK, D), jnp.bfloat16),
            pltpu.VMEM((1, D), jnp.float32),
            pltpu.VMEM((2, D), jnp.float32),
            pltpu.SemaphoreType.DMA((ROWS // STEP + 2,)),
        ],
        compiler_params=params(8 << 20),
        cost_estimate=cost(ROWS * D * 8, ROWS * D * 6),
    )(*map(in_hbm, (tokens, gain, mod)))


def project_into(x, w_ref, out_ref, at, width=256):
    rows = x.shape[0]
    for c in range(0, D, width):
        out_ref[at : at + rows, c : c + width] = jnp.dot(
            x, w_ref[:, c : c + width], preferred_element_type=jnp.float32
        ).astype(jnp.bfloat16)


def own_kernel(n, *refs):
    x_ref, hbms, refs = refs[0], refs[1:4], refs[4 + 2 * n :]
    out_refs, w_refs, sems = refs[:3], (refs[5], refs[3], refs[4]), refs[6]
    loads = [pltpu.make_async_copy(hbm, w, sems.at[i]) for i, (hbm, w) in enumerate(zip(hbms, w_refs))]
    for copy in loads[:2]:
        copy.start()
    for i, (w_ref, out_ref) in enumerate(zip(w_refs, out_refs)):
        loads[i].wait()
        if i + 2 < len(loads):
            loads[i + 2].start()
        project_into(x_ref[...], w_ref, out_ref, 0)


def own_project(x, weights, later=()):
    n = len(later)
    weight = pltpu.VMEM((D, D), jnp.bfloat16)
    out = pl.pallas_call(
        functools.partial(own_kernel, n),
        out_shape=[jax.ShapeDtypeStruct(c.shape, c.dtype) for c in later]
        + [pltpu.VMEM((ROWS, D), jnp.bfloat16)] * 3
        + [weight] * 2,
        in_specs=[VMEM] + [ANY] * 3 + [VMEM] * n,
        out_specs=[VMEM] * (n + 5),
        input_output_aliases={4 + i: i for i in range(n)},
        scratch_shapes=[weight, pltpu.SemaphoreType.DMA((3,))],
        compiler_params=params(12 << 20),
        cost_estimate=cost(6 * ROWS * D * D, 6 * D * D),
    )(x, *map(in_hbm, weights), *later)
    return out[:n], out[n : n + 3], out[n + 3 :]


def gate_kernel(*refs):
    pass


def gate(x, after):
    return pl.pallas_call(
        gate_kernel,
        out_shape=jax.ShapeDtypeStruct(x.shape, x.dtype),
        in_specs=[VMEM] * 2,
        out_specs=VMEM,
        input_output_aliases={0: 0},
        compiler_params=params(1 << 20),
    )(x, after)


def project_rows(x_refs, ats, pairs):
    x = jnp.concatenate([ref[...] for ref in x_refs], axis=0) if len(x_refs) > 1 else x_refs[0][...]
    for w_ref, out_ref in pairs:
        for c in range(0, D, 256):
            y = jnp.dot(x, w_ref[:, c : c + 256], preferred_element_type=jnp.float32).astype(jnp.bfloat16)
            row = 0
            for ref, at in zip(x_refs, ats):
                rows = ref.shape[0]
                out_ref[at : at + rows, c : c + 256] = y[row : row + rows]
                row += rows


def kv_kernel(ats, own, *refs):
    n = len(ats)
    wk_ref, wv_ref = refs[n : n + 2]
    k_ref, v_ref, token_ref = refs[n + 4 : n + 7]
    token_ref[...] = jnp.zeros_like(token_ref)
    copies = []
    if own:
        for i, (source, held_ref) in enumerate(zip(refs[n + 2 : n + 4], (k_ref, v_ref))):
            copies.append(pltpu.make_async_copy(source, held_ref.at[pl.ds(0, ROWS)], refs[-1].at[i]))
            copies[-1].start()
    project_rows(refs[:n], ats, ((wk_ref, k_ref), (wv_ref, v_ref)))
    for copy in copies:
        copy.wait()


def kv_project(xs, ats, wk, wv, held, own):
    n = len(xs)
    rows = sum(x.shape[0] for x in xs)
    shape = pltpu.VMEM((4 * ROWS, D), jnp.bfloat16)
    return pl.pallas_call(
        functools.partial(kv_kernel, ats, own),
        out_shape=[shape, shape, jax.ShapeDtypeStruct((8, 128), jnp.float32)],
        in_specs=[VMEM] * (n + 4),
        out_specs=[VMEM] * 3,
        input_output_aliases={} if own else {n + 2: 0, n + 3: 1},
        scratch_shapes=[pltpu.SemaphoreType.DMA((2,))] if own else [],
        compiler_params=params(8 << 20),
        cost_estimate=cost(4 * rows * D * D, 6 * D * D),
    )(*xs, wk, wv, *held)


def attend_kernel(ats, finish, *refs):
    refs = list(refs)

    def take(n):
        out = refs[:n]
        del refs[:n]
        return out

    x_refs = take(len(ats))
    wk_ref, wv_ref, q_ref, neigh_hbm, count_hbm, cross_hbm = take(6)
    take(2)
    if finish is not None:
        part_refs, (wo_hbm,) = take(2), take(1)
    if finish == 1:
        (first_ref,) = take(1)
    k_ref, v_ref = take(2)
    if finish is None:
        part_refs = take(2)
    else:
        (out_ref,) = take(1)
    neigh_ref, count_ref, cross_ref, sems = take(4)
    if finish is not None:
        wo_ref, att_ref = take(2)
    if finish == 1:
        (upd_ref,) = take(1)
    lists = [
        pltpu.make_async_copy(neigh_hbm, neigh_ref, sems.at[0]),
        pltpu.make_async_copy(count_hbm, count_ref, sems.at[1]),
        pltpu.make_async_copy(cross_hbm, cross_ref, sems.at[2]),
    ]
    for copy in lists:
        copy.start()
    if finish is not None:
        wo_copy = pltpu.make_async_copy(wo_hbm, wo_ref, sems.at[3])
        wo_copy.start()
    copies = []
    if finish == 1:
        copies.append(pltpu.make_async_copy(first_ref, out_ref.at[0], sems.at[4]))
        copies[0].start()
    project_rows(x_refs, ats, ((wk_ref, k_ref), (wv_ref, v_ref)))
    for copy in lists:
        copy.wait()
    mine = lax.axis_index("frame")
    odd = lax.axis_index("tile") % 2
    r = lax.broadcasted_iota(jnp.int32, (GW, GW), 0) // HEAD
    c = lax.broadcasted_iota(jnp.int32, (GW, GW), 1) // HEAD
    diagonal = r == c
    even_head = lax.broadcasted_iota(jnp.int32, (BT, 2 * HEAD), 1) < HEAD
    lane = lax.broadcasted_iota(jnp.int32, (1, NS * BT), 1) // BT

    def rows_of(block):
        return pl.ds(pl.multiple_of(block * BT, BT), BT)

    def near_slots(frame, b):
        found = []
        for s in range(NS):
            e = neigh_ref[0, b, s]
            side = e // NBLK
            core = jnp.where(side == 2, odd == 0, odd == 1)
            source = jnp.where(side == 1, 0, jnp.where(core, 2, 3))
            found.append(rows_of(source * (2 * NBLK) + frame * NBLK + (e - side * NBLK)))
        return found

    def far_slots(frame, b):
        found = []
        for s in range(CS):
            e = cross_ref[frame, 0, b, s]
            owner = e // (2 * NBLK)
            found.append(rows_of(e - owner * (2 * NBLK) + jnp.where(owner == mine, 0, 2 * NBLK)))
        return found

    def own_columns(x):
        halves = []
        for h in range(0, GROUP, 2):
            two = slice(h * HEAD, (h + 2) * HEAD) if x.shape[1] > 1 else slice(0, 1)
            halves.append(
                jnp.where(even_head, x[h * BT : (h + 1) * BT, two], x[(h + 1) * BT : (h + 2) * BT, two])
            )
        return jnp.concatenate(halves, axis=1)

    def part(frame, b, g, at, masked):
        u = frame * NBLK + b
        cols = slice(g * GW, (g + 1) * GW)
        q = q_ref[u * BT : (u + 1) * BT, cols]
        q4 = jnp.concatenate([q] * GROUP, axis=0)
        q4 = jnp.where(diagonal, q4, jnp.zeros_like(q4))
        keys = jnp.concatenate([k_ref[a, cols] for a in at], axis=0)
        values = jnp.concatenate([v_ref[a, cols] for a in at], axis=0)
        scores = lax.dot_general(
            q4, keys, (((1,), (1,)), ((), ())), preferred_element_type=jnp.float32
        )
        if masked:
            scores = scores + jnp.where(lane < count_ref[0, b], jnp.float32(0.0), jnp.float32(-1e30))
        peak = jnp.max(scores, axis=1, keepdims=True)
        weights = jnp.exp2((scores - peak) * EXP_SCALE)
        total = jnp.sum(weights, axis=1, keepdims=True)
        att = jnp.dot(weights.astype(jnp.bfloat16), values, preferred_element_type=jnp.float32)
        return own_columns(att), own_columns(peak), own_columns(total)

    def parts(frame, slots, masked):
        at = [slots(frame, b) for b in range(NBLK)]
        for g in range(D // GW):
            for b in range(NBLK):
                where = (slice(b * BT, (b + 1) * BT), slice(g * GW, (g + 1) * GW))
                yield where, part(frame, b, g, at[b], masked)

    if finish is None:
        for frame in range(2):
            for where, values in parts(frame, far_slots, False):
                att, peak, total = values
                part_refs[0][(frame, *where)] = att / total
                part_refs[1][(frame, *where)] = peak * EXP_SCALE + jnp.log2(total)
        return
    for where, (att, peak, total) in parts(finish, near_slots, True):
        far, level = (ref[(finish, *where)] for ref in part_refs)
        scale = jnp.exp2(jnp.minimum(peak * EXP_SCALE - level, FAR_AHEAD))
        att_ref[where] = ((far + att * scale) / (1.0 + total * scale)).astype(jnp.bfloat16)
    wo_copy.wait()
    if finish == 0:
        project_into(att_ref[...], wo_ref, out_ref, 0)
        return
    for i, col in enumerate(range(0, D, 256)):
        cols = slice(col, col + 256)
        upd_ref[:, cols] = jnp.dot(
            att_ref[...], wo_ref[:, cols], preferred_element_type=jnp.float32
        ).astype(jnp.bfloat16)
        some = pl.ds(col, 256)
        copies.append(pltpu.make_async_copy(upd_ref.at[:, some], out_ref.at[1, :, some], sems.at[5 + i]))
        copies[-1].start()
    for copy in copies:
        copy.wait()


def attend(xs, ats, wk, wv, held, queries, lists, finish=None, parts=(), w_out=None, first=None):
    n = len(xs)
    held_shape = pltpu.VMEM((4 * ROWS, D), jnp.bfloat16)
    args = [*xs, wk, wv, queries, *lists, *held]
    in_specs = [VMEM] * (n + 3) + [ANY] * 3 + [VMEM] * 2
    out_shape, out_specs = [held_shape] * 2, [VMEM] * 2
    aliases = {n + 6: 0, n + 7: 1}
    scratch = [pltpu.SMEM(x.shape, jnp.int32) for x in lists] + [pltpu.SemaphoreType.DMA((9,))]
    rows = pltpu.VMEM((TOK, D), jnp.bfloat16)
    if finish is None:
        out_shape += [jax.ShapeDtypeStruct((2, TOK, D), jnp.float32)] * 2
        out_specs += [VMEM] * 2
    else:
        args += [*parts, in_hbm(w_out)]
        in_specs += [VMEM] * 2 + [ANY]
        scratch += [pltpu.VMEM((D, D), jnp.bfloat16), rows]
    if finish == 0:
        out_shape.append(rows)
        out_specs.append(VMEM)
    if finish == 1:
        args.append(first)
        in_specs.append(VMEM)
        out_shape.append(jax.ShapeDtypeStruct((2, TOK, D), jnp.bfloat16))
        out_specs.append(ANY)
        scratch.append(rows)
    return pl.pallas_call(
        functools.partial(attend_kernel, ats, finish),
        out_shape=out_shape,
        in_specs=in_specs,
        out_specs=out_specs,
        scratch_shapes=scratch,
        input_output_aliases=aliases,
        compiler_params=params(16 << 20),
        cost_estimate=cost(2 * TOK * D * D + 16 * TOK * SLOTS * BT * D, 8 * D * D),
    )(*args)


def local(tokens, norm_gain, modulation, w_query, w_key, w_value, w_out, neigh_list, neigh_count, cross_list):
    tiles = lax.axis_size("tile")

    def device(f, t):
        return f * tiles + t % tiles

    cells = [(f, t) for f in range(2) for t in range(tiles)]
    partner = [(device(f, t), device(1 - f, t)) for f, t in cells]
    pair = [(device(f, t), device(f, t ^ 1)) for f, t in cells]
    onward = [(device(f, t), device(1 - f, t + 1 if t % 2 else t - 1)) for f, t in cells]

    def swap(x):
        return lax.ppermute(x, BOTH, partner)

    def cross(x):
        return lax.ppermute(x, BOTH, pair)

    def forward(x):
        return lax.ppermute(x, BOTH, onward)

    def at(source, i):
        return source * ROWS + i * CR

    lists = (neigh_list, neigh_count, cross_list)
    whole, *chunks = norm(tokens, norm_gain[None], modulation)
    s0, s1 = swap(chunks[0]), swap(chunks[1])
    across = cross(whole)
    later, (queries, *own), (wk, wv) = own_project(whole, [w_query, w_key, w_value], [chunks[2]])
    s2 = swap(later[0])
    o0 = forward(s0)
    *held, token = kv_project([s0, across], [at(1, 0), 2 * ROWS], wk, wv, own, True)
    s1 = gate(s1, token)
    o1 = forward(s1)
    *held, token = kv_project([s1], [at(1, 1)], wk, wv, held, False)
    s2 = gate(s2, token)
    o2 = forward(s2)
    *held, far, level = attend([s2], [at(1, 2)], wk, wv, held, queries, lists)
    parts = far, level
    *held, first = attend([o0, o1], [at(3, 0), at(3, 1)], wk, wv, held, queries, lists, 0, parts, w_out)
    return attend([o2], [at(3, 2)], wk, wv, held, queries, lists, 1, parts, w_out, first)[2]


def solution(mesh):
    return jax.shard_map(
        local,
        mesh=mesh,
        in_specs=(
            P("frame", "tile", None),
            P(),
            P("frame", None),
            P(),
            P(),
            P(),
            P(),
            P("tile", None, None),
            P("tile", None),
            P("frame", "tile", None, None),
        ),
        out_specs=P("frame", "tile", None),
        check_vma=False,
    )
```

```python
import functools
import math

import jax
import jax.numpy as jnp
import numpy as np
from jax import lax
from jax.experimental import pallas as pl
from jax.experimental.pallas import tpu as pltpu
from jax.sharding import PartitionSpec as P

HEADS = 16
NS = 6
CS = 4
SLOTS = NS + CS
BT = 64
NBLK = 3
D = 1024
HEAD = D // HEADS
GROUP = 4
GW = GROUP * HEAD
TOK = NBLK * BT
ROWS = 2 * TOK
CHUNKS = 3
CR = ROWS // CHUNKS
STEP = math.gcd(CR, TOK)
BOTH = ("frame", "tile")
VMEM = pl.BlockSpec(memory_space=pltpu.VMEM)
ANY = pl.BlockSpec(memory_space=pl.ANY)
FAR_AHEAD = 64.0
EXP_SCALE = float(np.log2(np.e) / np.sqrt(HEAD))


def params(limit):
    return pltpu.CompilerParams(vmem_limit_bytes=limit)


def in_hbm(x):
    return pltpu.with_memory_space_constraint(x, pltpu.HBM)


def cost(flops, nbytes):
    return pl.CostEstimate(flops=int(flops), bytes_accessed=int(nbytes), transcendentals=0)


def norm_kernel(tok_hbm, gain_hbm, mod_hbm, whole_ref, *rest):
    chunk_refs, (tok_ref, gain_ref, mod_ref, sems) = rest[:CHUNKS], rest[CHUNKS:]
    side = [
        pltpu.make_async_copy(gain_hbm, gain_ref, sems.at[2]),
        pltpu.make_async_copy(mod_hbm, mod_ref, sems.at[3]),
    ]
    loads = [pltpu.make_async_copy(tok_hbm.at[f], tok_ref.at[f], sems.at[f]) for f in range(2)]
    for copy in loads[:1] + side + loads[1:]:
        copy.start()
    for copy in side:
        copy.wait()
    for i in range(ROWS // STEP):
        frame, row = divmod(i * STEP, TOK)
        if row == 0:
            loads[frame].wait()
        x = tok_ref[frame, row : row + STEP, :].astype(jnp.float32)
        meansq = jnp.mean(x * x, axis=-1, keepdims=True)
        scaled = x * lax.rsqrt(meansq + 1e-06) * gain_ref[...] * (1.0 + mod_ref[frame : frame + 1, :])
        normed = scaled.astype(jnp.bfloat16)
        whole_ref[i * STEP : (i + 1) * STEP, :] = normed
        chunk, row = divmod(i * STEP, CR)
        chunk_refs[chunk][row : row + STEP, :] = normed


def norm(tokens, gain, mod):
    chunk = jax.ShapeDtypeStruct((CR, D), jnp.bfloat16)
    return pl.pallas_call(
        norm_kernel,
        out_shape=[jax.ShapeDtypeStruct((ROWS, D), jnp.bfloat16)] + [chunk] * CHUNKS,
        in_specs=[ANY] * 3,
        out_specs=[VMEM] * (1 + CHUNKS),
        scratch_shapes=[
            pltpu.VMEM((2, TOK, D), jnp.bfloat16),
            pltpu.VMEM((1, D), jnp.float32),
            pltpu.VMEM((2, D), jnp.float32),
            pltpu.SemaphoreType.DMA((4,)),
        ],
        compiler_params=params(8 << 20),
        cost_estimate=cost(ROWS * D * 8, ROWS * D * 6),
    )(*map(in_hbm, (tokens, gain, mod)))


def project_into(x, w_ref, out_ref, at, width=256):
    rows = x.shape[0]
    for c in range(0, D, width):
        out_ref[at : at + rows, c : c + width] = jnp.dot(
            x, w_ref[:, c : c + width], preferred_element_type=jnp.float32
        ).astype(jnp.bfloat16)


def own_kernel(n, *refs):
    x_ref, hbms, refs = refs[0], refs[1:4], refs[4 + 2 * n :]
    out_refs, w_refs, sems = refs[:3], (refs[5], refs[3], refs[4]), refs[6]
    loads = [pltpu.make_async_copy(hbm, w, sems.at[i]) for i, (hbm, w) in enumerate(zip(hbms, w_refs))]
    for copy in loads[:2]:
        copy.start()
    for i, (w_ref, out_ref) in enumerate(zip(w_refs, out_refs)):
        loads[i].wait()
        if i + 2 < len(loads):
            loads[i + 2].start()
        project_into(x_ref[...], w_ref, out_ref, 0)


def own_project(x, weights, later=()):
    n = len(later)
    weight = pltpu.VMEM((D, D), jnp.bfloat16)
    out = pl.pallas_call(
        functools.partial(own_kernel, n),
        out_shape=[jax.ShapeDtypeStruct(c.shape, c.dtype) for c in later]
        + [pltpu.VMEM((ROWS, D), jnp.bfloat16)] * 3
        + [weight] * 2,
        in_specs=[VMEM] + [ANY] * 3 + [VMEM] * n,
        out_specs=[VMEM] * (n + 5),
        input_output_aliases={4 + i: i for i in range(n)},
        scratch_shapes=[weight, pltpu.SemaphoreType.DMA((3,))],
        compiler_params=params(12 << 20),
        cost_estimate=cost(6 * ROWS * D * D, 6 * D * D),
    )(x, *map(in_hbm, weights), *later)
    return out[:n], out[n : n + 3], out[n + 3 :]


def gate_kernel(*refs):
    pass


def gate(x, after):
    return pl.pallas_call(
        gate_kernel,
        out_shape=jax.ShapeDtypeStruct(x.shape, x.dtype),
        in_specs=[VMEM] * 2,
        out_specs=VMEM,
        input_output_aliases={0: 0},
        compiler_params=params(1 << 20),
    )(x, after)


def project_rows(x_refs, ats, pairs):
    x = jnp.concatenate([ref[...] for ref in x_refs], axis=0) if len(x_refs) > 1 else x_refs[0][...]
    for w_ref, out_ref in pairs:
        for c in range(0, D, 256):
            y = jnp.dot(x, w_ref[:, c : c + 256], preferred_element_type=jnp.float32).astype(jnp.bfloat16)
            row = 0
            for ref, at in zip(x_refs, ats):
                rows = ref.shape[0]
                out_ref[at : at + rows, c : c + 256] = y[row : row + rows]
                row += rows


def kv_kernel(ats, own, *refs):
    n = len(ats)
    wk_ref, wv_ref = refs[n : n + 2]
    k_ref, v_ref, token_ref = refs[n + 4 : n + 7]
    token_ref[...] = jnp.zeros_like(token_ref)
    copies = []
    if own:
        for i, (source, held_ref) in enumerate(zip(refs[n + 2 : n + 4], (k_ref, v_ref))):
            copies.append(pltpu.make_async_copy(source, held_ref.at[pl.ds(0, ROWS)], refs[-1].at[i]))
            copies[-1].start()
    project_rows(refs[:n], ats, ((wk_ref, k_ref), (wv_ref, v_ref)))
    for copy in copies:
        copy.wait()


def kv_project(xs, ats, wk, wv, held, own):
    n = len(xs)
    rows = sum(x.shape[0] for x in xs)
    shape = pltpu.VMEM((4 * ROWS, D), jnp.bfloat16)
    return pl.pallas_call(
        functools.partial(kv_kernel, ats, own),
        out_shape=[shape, shape, jax.ShapeDtypeStruct((8, 128), jnp.float32)],
        in_specs=[VMEM] * (n + 4),
        out_specs=[VMEM] * 3,
        input_output_aliases={} if own else {n + 2: 0, n + 3: 1},
        scratch_shapes=[pltpu.SemaphoreType.DMA((2,))] if own else [],
        compiler_params=params(8 << 20),
        cost_estimate=cost(4 * rows * D * D, 6 * D * D),
    )(*xs, wk, wv, *held)


def attend_kernel(ats, finish, *refs):
    refs = list(refs)

    def take(n):
        out = refs[:n]
        del refs[:n]
        return out

    x_refs = take(len(ats))
    wk_ref, wv_ref, q_ref, neigh_hbm, count_hbm, cross_hbm = take(6)
    take(2)
    if finish is not None:
        part_refs, (wo_hbm,) = take(2), take(1)
    if finish == 1:
        (first_ref,) = take(1)
    k_ref, v_ref = take(2)
    if finish is None:
        part_refs = take(2)
    else:
        (out_ref,) = take(1)
    neigh_ref, count_ref, cross_ref, sems = take(4)
    if finish is not None:
        wo_ref, att_ref = take(2)
    if finish == 1:
        (upd_ref,) = take(1)
    lists = [
        pltpu.make_async_copy(neigh_hbm, neigh_ref, sems.at[0]),
        pltpu.make_async_copy(count_hbm, count_ref, sems.at[1]),
        pltpu.make_async_copy(cross_hbm, cross_ref, sems.at[2]),
    ]
    for copy in lists:
        copy.start()
    if finish is not None:
        wo_copy = pltpu.make_async_copy(wo_hbm, wo_ref, sems.at[3])
        wo_copy.start()
    copies = []
    if finish == 1:
        copies.append(pltpu.make_async_copy(first_ref, out_ref.at[0], sems.at[4]))
        copies[0].start()
    project_rows(x_refs, ats, ((wk_ref, k_ref), (wv_ref, v_ref)))
    for copy in lists:
        copy.wait()
    mine = lax.axis_index("frame")
    odd = lax.axis_index("tile") % 2
    r = lax.broadcasted_iota(jnp.int32, (GW, GW), 0) // HEAD
    c = lax.broadcasted_iota(jnp.int32, (GW, GW), 1) // HEAD
    diagonal = r == c
    even_head = lax.broadcasted_iota(jnp.int32, (BT, 2 * HEAD), 1) < HEAD
    lane = lax.broadcasted_iota(jnp.int32, (1, NS * BT), 1) // BT

    def rows_of(block):
        return pl.ds(pl.multiple_of(block * BT, BT), BT)

    def near_slots(frame, b):
        found = []
        for s in range(NS):
            e = neigh_ref[0, b, s]
            side = e // NBLK
            core = jnp.where(side == 2, odd == 0, odd == 1)
            source = jnp.where(side == 1, 0, jnp.where(core, 2, 3))
            found.append(rows_of(source * (2 * NBLK) + frame * NBLK + (e - side * NBLK)))
        return found

    def far_slots(frame, b):
        found = []
        for s in range(CS):
            e = cross_ref[frame, 0, b, s]
            owner = e // (2 * NBLK)
            found.append(rows_of(e - owner * (2 * NBLK) + jnp.where(owner == mine, 0, 2 * NBLK)))
        return found

    def own_columns(x):
        halves = []
        for h in range(0, GROUP, 2):
            two = slice(h * HEAD, (h + 2) * HEAD) if x.shape[1] > 1 else slice(0, 1)
            halves.append(
                jnp.where(even_head, x[h * BT : (h + 1) * BT, two], x[(h + 1) * BT : (h + 2) * BT, two])
            )
        return jnp.concatenate(halves, axis=1)

    def part(frame, b, g, at, masked):
        u = frame * NBLK + b
        cols = slice(g * GW, (g + 1) * GW)
        q = q_ref[u * BT : (u + 1) * BT, cols]
        q4 = jnp.concatenate([q] * GROUP, axis=0)
        q4 = jnp.where(diagonal, q4, jnp.zeros_like(q4))
        keys = jnp.concatenate([k_ref[a, cols] for a in at], axis=0)
        values = jnp.concatenate([v_ref[a, cols] for a in at], axis=0)
        scores = lax.dot_general(
            q4, keys, (((1,), (1,)), ((), ())), preferred_element_type=jnp.float32
        )
        if masked:
            scores = scores + jnp.where(lane < count_ref[0, b], jnp.float32(0.0), jnp.float32(-1e30))
        peak = jnp.max(scores, axis=1, keepdims=True)
        weights = jnp.exp2((scores - peak) * EXP_SCALE)
        total = jnp.sum(weights, axis=1, keepdims=True)
        att = jnp.dot(weights.astype(jnp.bfloat16), values, preferred_element_type=jnp.float32)
        return own_columns(att), own_columns(peak), own_columns(total)

    def parts(frame, slots, masked):
        at = [slots(frame, b) for b in range(NBLK)]
        for b in range(NBLK):
            for g in range(D // GW):
                where = (slice(b * BT, (b + 1) * BT), slice(g * GW, (g + 1) * GW))
                yield where, part(frame, b, g, at[b], masked)

    if finish is None:
        for frame in range(2):
            for where, values in parts(frame, far_slots, False):
                att, peak, total = values
                part_refs[0][(frame, *where)] = att / total
                part_refs[1][(frame, *where)] = peak * EXP_SCALE + jnp.log2(total)
        return
    for where, (att, peak, total) in parts(finish, near_slots, True):
        far, level = (ref[(finish, *where)] for ref in part_refs)
        scale = jnp.exp2(jnp.minimum(peak * EXP_SCALE - level, FAR_AHEAD))
        att_ref[where] = ((far + att * scale) / (1.0 + total * scale)).astype(jnp.bfloat16)
    wo_copy.wait()
    if finish == 0:
        project_into(att_ref[...], wo_ref, out_ref, 0)
        return
    for i, col in enumerate(range(0, D, 256)):
        cols = slice(col, col + 256)
        upd_ref[:, cols] = jnp.dot(
            att_ref[...], wo_ref[:, cols], preferred_element_type=jnp.float32
        ).astype(jnp.bfloat16)
        some = pl.ds(col, 256)
        copies.append(pltpu.make_async_copy(upd_ref.at[:, some], out_ref.at[1, :, some], sems.at[5 + i]))
        copies[-1].start()
    for copy in copies:
        copy.wait()


def attend(xs, ats, wk, wv, held, queries, lists, finish=None, parts=(), w_out=None, first=None):
    n = len(xs)
    held_shape = pltpu.VMEM((4 * ROWS, D), jnp.bfloat16)
    args = [*xs, wk, wv, queries, *lists, *held]
    in_specs = [VMEM] * (n + 3) + [ANY] * 3 + [VMEM] * 2
    out_shape, out_specs = [held_shape] * 2, [VMEM] * 2
    aliases = {n + 6: 0, n + 7: 1}
    scratch = [pltpu.SMEM(x.shape, jnp.int32) for x in lists] + [pltpu.SemaphoreType.DMA((9,))]
    rows = pltpu.VMEM((TOK, D), jnp.bfloat16)
    if finish is None:
        out_shape += [jax.ShapeDtypeStruct((2, TOK, D), jnp.float32)] * 2
        out_specs += [VMEM] * 2
    else:
        args += [*parts, in_hbm(w_out)]
        in_specs += [VMEM] * 2 + [ANY]
        scratch += [pltpu.VMEM((D, D), jnp.bfloat16), rows]
    if finish == 0:
        out_shape.append(rows)
        out_specs.append(VMEM)
    if finish == 1:
        args.append(first)
        in_specs.append(VMEM)
        out_shape.append(jax.ShapeDtypeStruct((2, TOK, D), jnp.bfloat16))
        out_specs.append(ANY)
        scratch.append(rows)
    return pl.pallas_call(
        functools.partial(attend_kernel, ats, finish),
        out_shape=out_shape,
        in_specs=in_specs,
        out_specs=out_specs,
        scratch_shapes=scratch,
        input_output_aliases=aliases,
        compiler_params=params(16 << 20),
        cost_estimate=cost(2 * TOK * D * D + 16 * TOK * SLOTS * BT * D, 8 * D * D),
    )(*args)


def local(tokens, norm_gain, modulation, w_query, w_key, w_value, w_out, neigh_list, neigh_count, cross_list):
    tiles = lax.axis_size("tile")

    def device(f, t):
        return f * tiles + t % tiles

    cells = [(f, t) for f in range(2) for t in range(tiles)]
    partner = [(device(f, t), device(1 - f, t)) for f, t in cells]
    pair = [(device(f, t), device(f, t ^ 1)) for f, t in cells]
    onward = [(device(f, t), device(1 - f, t + 1 if t % 2 else t - 1)) for f, t in cells]

    def swap(x):
        return lax.ppermute(x, BOTH, partner)

    def cross(x):
        return lax.ppermute(x, BOTH, pair)

    def forward(x):
        return lax.ppermute(x, BOTH, onward)

    def at(source, i):
        return source * ROWS + i * CR

    lists = (neigh_list, neigh_count, cross_list)
    whole, *chunks = norm(tokens, norm_gain[None], modulation)
    s0, s1 = swap(chunks[0]), swap(chunks[1])
    across = cross(whole)
    later, (queries, *own), (wk, wv) = own_project(whole, [w_query, w_key, w_value], [chunks[2]])
    s2 = swap(later[0])
    o0 = forward(s0)
    *held, token = kv_project([s0, across], [at(1, 0), 2 * ROWS], wk, wv, own, True)
    s1 = gate(s1, token)
    o1 = forward(s1)
    *held, token = kv_project([s1], [at(1, 1)], wk, wv, held, False)
    s2 = gate(s2, token)
    o2 = forward(s2)
    *held, far, level = attend([s2], [at(1, 2)], wk, wv, held, queries, lists)
    parts = far, level
    *held, first = attend([o0, o1], [at(3, 0), at(3, 1)], wk, wv, held, queries, lists, 0, parts, w_out)
    return attend([o2], [at(3, 2)], wk, wv, held, queries, lists, 1, parts, w_out, first)[2]


def solution(mesh):
    return jax.shard_map(
        local,
        mesh=mesh,
        in_specs=(
            P("frame", "tile", None),
            P(),
            P("frame", None),
            P(),
            P(),
            P(),
            P(),
            P("tile", None, None),
            P("tile", None),
            P("frame", "tile", None, None),
        ),
        out_specs=P("frame", "tile", None),
        check_vma=False,
    )
```

```python
import functools
import math

import jax
import jax.numpy as jnp
import numpy as np
from jax import lax
from jax.experimental import pallas as pl
from jax.experimental.pallas import tpu as pltpu
from jax.sharding import PartitionSpec as P

HEADS = 16
NS = 6
CS = 4
SLOTS = NS + CS
BT = 64
NBLK = 3
D = 1024
HEAD = D // HEADS
GROUP = 4
GW = GROUP * HEAD
TOK = NBLK * BT
ROWS = 2 * TOK
CHUNKS = 3
CR = ROWS // CHUNKS
STEP = math.gcd(CR, TOK)
BOTH = ("frame", "tile")
VMEM = pl.BlockSpec(memory_space=pltpu.VMEM)
ANY = pl.BlockSpec(memory_space=pl.ANY)
FAR_AHEAD = 64.0
EXP_SCALE = float(np.log2(np.e) / np.sqrt(HEAD))


def params(limit):
    return pltpu.CompilerParams(vmem_limit_bytes=limit)


def in_hbm(x):
    return pltpu.with_memory_space_constraint(x, pltpu.HBM)


def cost(flops, nbytes):
    return pl.CostEstimate(flops=int(flops), bytes_accessed=int(nbytes), transcendentals=0)


def norm_kernel(tok_hbm, gain_hbm, mod_hbm, whole_ref, *rest):
    chunk_refs, (tok_ref, gain_ref, mod_ref, sems) = rest[:CHUNKS], rest[CHUNKS:]
    side = [
        pltpu.make_async_copy(gain_hbm, gain_ref, sems.at[2]),
        pltpu.make_async_copy(mod_hbm, mod_ref, sems.at[3]),
    ]
    loads = [pltpu.make_async_copy(tok_hbm.at[f], tok_ref.at[f], sems.at[f]) for f in range(2)]
    for copy in loads[:1] + side + loads[1:]:
        copy.start()
    for copy in side:
        copy.wait()
    for i in range(ROWS // STEP):
        frame, row = divmod(i * STEP, TOK)
        if row == 0:
            loads[frame].wait()
        x = tok_ref[frame, row : row + STEP, :].astype(jnp.float32)
        meansq = jnp.mean(x * x, axis=-1, keepdims=True)
        scaled = x * lax.rsqrt(meansq + 1e-06) * gain_ref[...] * (1.0 + mod_ref[frame : frame + 1, :])
        normed = scaled.astype(jnp.bfloat16)
        whole_ref[i * STEP : (i + 1) * STEP, :] = normed
        chunk, row = divmod(i * STEP, CR)
        chunk_refs[chunk][row : row + STEP, :] = normed


def norm(tokens, gain, mod):
    chunk = jax.ShapeDtypeStruct((CR, D), jnp.bfloat16)
    return pl.pallas_call(
        norm_kernel,
        out_shape=[jax.ShapeDtypeStruct((ROWS, D), jnp.bfloat16)] + [chunk] * CHUNKS,
        in_specs=[ANY] * 3,
        out_specs=[VMEM] * (1 + CHUNKS),
        scratch_shapes=[
            pltpu.VMEM((2, TOK, D), jnp.bfloat16),
            pltpu.VMEM((1, D), jnp.float32),
            pltpu.VMEM((2, D), jnp.float32),
            pltpu.SemaphoreType.DMA((4,)),
        ],
        compiler_params=params(8 << 20),
        cost_estimate=cost(ROWS * D * 8, ROWS * D * 6),
    )(*map(in_hbm, (tokens, gain, mod)))


def project_into(x, w_ref, out_ref, at, width=256):
    rows = x.shape[0]
    for c in range(0, D, width):
        out_ref[at : at + rows, c : c + width] = jnp.dot(
            x, w_ref[:, c : c + width], preferred_element_type=jnp.float32
        ).astype(jnp.bfloat16)


def own_kernel(n, *refs):
    x_ref, hbms, refs = refs[0], refs[1:4], refs[4 + 2 * n :]
    out_refs, w_refs, sems = refs[:3], (refs[5], refs[3], refs[4]), refs[6]
    loads = [pltpu.make_async_copy(hbm, w, sems.at[i]) for i, (hbm, w) in enumerate(zip(hbms, w_refs))]
    for copy in loads[:2]:
        copy.start()
    for i, (w_ref, out_ref) in enumerate(zip(w_refs, out_refs)):
        loads[i].wait()
        if i + 2 < len(loads):
            loads[i + 2].start()
        project_into(x_ref[...], w_ref, out_ref, 0)


def own_project(x, weights, later=()):
    n = len(later)
    weight = pltpu.VMEM((D, D), jnp.bfloat16)
    out = pl.pallas_call(
        functools.partial(own_kernel, n),
        out_shape=[jax.ShapeDtypeStruct(c.shape, c.dtype) for c in later]
        + [pltpu.VMEM((ROWS, D), jnp.bfloat16)] * 3
        + [weight] * 2,
        in_specs=[VMEM] + [ANY] * 3 + [VMEM] * n,
        out_specs=[VMEM] * (n + 5),
        input_output_aliases={4 + i: i for i in range(n)},
        scratch_shapes=[weight, pltpu.SemaphoreType.DMA((3,))],
        compiler_params=params(12 << 20),
        cost_estimate=cost(6 * ROWS * D * D, 6 * D * D),
    )(x, *map(in_hbm, weights), *later)
    return out[:n], out[n : n + 3], out[n + 3 :]


def gate_kernel(*refs):
    pass


def gate(x, after):
    return pl.pallas_call(
        gate_kernel,
        out_shape=jax.ShapeDtypeStruct(x.shape, x.dtype),
        in_specs=[VMEM] * 2,
        out_specs=VMEM,
        input_output_aliases={0: 0},
        compiler_params=params(1 << 20),
    )(x, after)


def project_rows(x_refs, ats, pairs):
    x = jnp.concatenate([ref[...] for ref in x_refs], axis=0) if len(x_refs) > 1 else x_refs[0][...]
    for w_ref, out_ref in pairs:
        for c in range(0, D, 256):
            y = jnp.dot(x, w_ref[:, c : c + 256], preferred_element_type=jnp.float32).astype(jnp.bfloat16)
            row = 0
            for ref, at in zip(x_refs, ats):
                rows = ref.shape[0]
                out_ref[at : at + rows, c : c + 256] = y[row : row + rows]
                row += rows


def kv_kernel(ats, own, *refs):
    n = len(ats)
    wk_ref, wv_ref = refs[n : n + 2]
    k_ref, v_ref, token_ref = refs[n + 4 : n + 7]
    token_ref[...] = jnp.zeros_like(token_ref)
    copies = []
    if own:
        for i, (source, held_ref) in enumerate(zip(refs[n + 2 : n + 4], (k_ref, v_ref))):
            copies.append(pltpu.make_async_copy(source, held_ref.at[pl.ds(0, ROWS)], refs[-1].at[i]))
            copies[-1].start()
    project_rows(refs[:n], ats, ((wk_ref, k_ref), (wv_ref, v_ref)))
    for copy in copies:
        copy.wait()


def kv_project(xs, ats, wk, wv, held, own):
    n = len(xs)
    rows = sum(x.shape[0] for x in xs)
    shape = pltpu.VMEM((4 * ROWS, D), jnp.bfloat16)
    return pl.pallas_call(
        functools.partial(kv_kernel, ats, own),
        out_shape=[shape, shape, jax.ShapeDtypeStruct((8, 128), jnp.float32)],
        in_specs=[VMEM] * (n + 4),
        out_specs=[VMEM] * 3,
        input_output_aliases={} if own else {n + 2: 0, n + 3: 1},
        scratch_shapes=[pltpu.SemaphoreType.DMA((2,))] if own else [],
        compiler_params=params(8 << 20),
        cost_estimate=cost(4 * rows * D * D, 6 * D * D),
    )(*xs, wk, wv, *held)


def attend_kernel(ats, finish, *refs):
    refs = list(refs)

    def take(n):
        out = refs[:n]
        del refs[:n]
        return out

    x_refs = take(len(ats))
    wk_ref, wv_ref, q_ref, neigh_hbm, count_hbm, cross_hbm = take(6)
    take(2)
    if finish is not None:
        part_refs, (wo_hbm,) = take(3), take(1)
    if finish == 1:
        (first_ref,) = take(1)
    k_ref, v_ref = take(2)
    if finish is None:
        part_refs = take(3)
    else:
        (out_ref,) = take(1)
    neigh_ref, count_ref, cross_ref, sems = take(4)
    if finish is not None:
        wo_ref, att_ref = take(2)
    if finish == 1:
        (upd_ref,) = take(1)
    lists = [
        pltpu.make_async_copy(neigh_hbm, neigh_ref, sems.at[0]),
        pltpu.make_async_copy(count_hbm, count_ref, sems.at[1]),
        pltpu.make_async_copy(cross_hbm, cross_ref, sems.at[2]),
    ]
    for copy in lists:
        copy.start()
    if finish is not None:
        wo_copy = pltpu.make_async_copy(wo_hbm, wo_ref, sems.at[3])
        wo_copy.start()
    copies = []
    if finish == 1:
        copies.append(pltpu.make_async_copy(first_ref, out_ref.at[0], sems.at[4]))
        copies[0].start()
    project_rows(x_refs, ats, ((wk_ref, k_ref), (wv_ref, v_ref)))
    for copy in lists:
        copy.wait()
    mine = lax.axis_index("frame")
    odd = lax.axis_index("tile") % 2
    r = lax.broadcasted_iota(jnp.int32, (GW, GW), 0) // HEAD
    c = lax.broadcasted_iota(jnp.int32, (GW, GW), 1) // HEAD
    diagonal = r == c
    even_head = lax.broadcasted_iota(jnp.int32, (BT, 2 * HEAD), 1) < HEAD
    lane = lax.broadcasted_iota(jnp.int32, (1, NS * BT), 1) // BT

    def rows_of(block):
        return pl.ds(pl.multiple_of(block * BT, BT), BT)

    def near_slots(frame, b):
        found = []
        for s in range(NS):
            e = neigh_ref[0, b, s]
            side = e // NBLK
            core = jnp.where(side == 2, odd == 0, odd == 1)
            source = jnp.where(side == 1, 0, jnp.where(core, 2, 3))
            found.append(rows_of(source * (2 * NBLK) + frame * NBLK + (e - side * NBLK)))
        return found

    def far_slots(frame, b):
        found = []
        for s in range(CS):
            e = cross_ref[frame, 0, b, s]
            owner = e // (2 * NBLK)
            found.append(rows_of(e - owner * (2 * NBLK) + jnp.where(owner == mine, 0, 2 * NBLK)))
        return found

    def own_columns(x):
        halves = []
        for h in range(0, GROUP, 2):
            two = slice(h * HEAD, (h + 2) * HEAD) if x.shape[1] > 1 else slice(0, 1)
            halves.append(
                jnp.where(even_head, x[h * BT : (h + 1) * BT, two], x[(h + 1) * BT : (h + 2) * BT, two])
            )
        return jnp.concatenate(halves, axis=1)

    def part(frame, b, g, at, masked):
        u = frame * NBLK + b
        cols = slice(g * GW, (g + 1) * GW)
        q = q_ref[u * BT : (u + 1) * BT, cols]
        q4 = jnp.concatenate([q] * GROUP, axis=0)
        q4 = jnp.where(diagonal, q4, jnp.zeros_like(q4))
        keys = jnp.concatenate([k_ref[a, cols] for a in at], axis=0)
        values = jnp.concatenate([v_ref[a, cols] for a in at], axis=0)
        scores = lax.dot_general(
            q4, keys, (((1,), (1,)), ((), ())), preferred_element_type=jnp.float32
        )
        if masked:
            scores = scores + jnp.where(lane < count_ref[0, b], jnp.float32(0.0), jnp.float32(-1e30))
        peak = jnp.max(scores, axis=1, keepdims=True)
        weights = jnp.exp2((scores - peak) * EXP_SCALE)
        total = jnp.sum(weights, axis=1, keepdims=True)
        att = jnp.dot(weights.astype(jnp.bfloat16), values, preferred_element_type=jnp.float32)
        return own_columns(att), own_columns(peak), own_columns(total)

    def parts(frame, slots, masked):
        at = [slots(frame, b) for b in range(NBLK)]
        for b in range(NBLK):
            for g in range(D // GW):
                where = (slice(b * BT, (b + 1) * BT), slice(g * GW, (g + 1) * GW))
                yield where, part(frame, b, g, at[b], masked)

    if finish is None:
        for frame in range(2):
            for where, values in parts(frame, far_slots, False):
                att, peak, total = values
                for ref, value in zip(part_refs, (att, peak, total)):
                    ref[(frame, *where)] = value
        return
    for where, (att, peak, total) in parts(finish, near_slots, True):
        att2, peak2, total2 = (ref[(finish, *where)] for ref in part_refs)
        scale = jnp.exp2(jnp.minimum((peak - peak2) * EXP_SCALE, FAR_AHEAD))
        att_ref[where] = ((att2 + att * scale) / (total2 + total * scale)).astype(jnp.bfloat16)
    wo_copy.wait()
    if finish == 0:
        project_into(att_ref[...], wo_ref, out_ref, 0)
        return
    for i, col in enumerate(range(0, D, 256)):
        cols = slice(col, col + 256)
        upd_ref[:, cols] = jnp.dot(
            att_ref[...], wo_ref[:, cols], preferred_element_type=jnp.float32
        ).astype(jnp.bfloat16)
        some = pl.ds(col, 256)
        copies.append(pltpu.make_async_copy(upd_ref.at[:, some], out_ref.at[1, :, some], sems.at[5 + i]))
        copies[-1].start()
    for copy in copies:
        copy.wait()


def attend(xs, ats, wk, wv, held, queries, lists, finish=None, parts=(), w_out=None, first=None):
    n = len(xs)
    held_shape = pltpu.VMEM((4 * ROWS, D), jnp.bfloat16)
    args = [*xs, wk, wv, queries, *lists, *held]
    in_specs = [VMEM] * (n + 3) + [ANY] * 3 + [VMEM] * 2
    out_shape, out_specs = [held_shape] * 2, [VMEM] * 2
    aliases = {n + 6: 0, n + 7: 1}
    scratch = [pltpu.SMEM(x.shape, jnp.int32) for x in lists] + [pltpu.SemaphoreType.DMA((9,))]
    rows = pltpu.VMEM((TOK, D), jnp.bfloat16)
    if finish is None:
        out_shape += [jax.ShapeDtypeStruct((2, TOK, D), jnp.float32)] * 3
        out_specs += [VMEM] * 3
    else:
        args += [*parts, in_hbm(w_out)]
        in_specs += [VMEM] * 3 + [ANY]
        scratch += [pltpu.VMEM((D, D), jnp.bfloat16), rows]
    if finish == 0:
        out_shape.append(rows)
        out_specs.append(VMEM)
    if finish == 1:
        args.append(first)
        in_specs.append(VMEM)
        out_shape.append(jax.ShapeDtypeStruct((2, TOK, D), jnp.bfloat16))
        out_specs.append(ANY)
        scratch.append(rows)
    return pl.pallas_call(
        functools.partial(attend_kernel, ats, finish),
        out_shape=out_shape,
        in_specs=in_specs,
        out_specs=out_specs,
        scratch_shapes=scratch,
        input_output_aliases=aliases,
        compiler_params=params(16 << 20),
        cost_estimate=cost(2 * TOK * D * D + 16 * TOK * SLOTS * BT * D, 8 * D * D),
    )(*args)


def local(tokens, norm_gain, modulation, w_query, w_key, w_value, w_out, neigh_list, neigh_count, cross_list):
    tiles = lax.axis_size("tile")

    def device(f, t):
        return f * tiles + t % tiles

    cells = [(f, t) for f in range(2) for t in range(tiles)]
    partner = [(device(f, t), device(1 - f, t)) for f, t in cells]
    pair = [(device(f, t), device(f, t ^ 1)) for f, t in cells]
    onward = [(device(f, t), device(1 - f, t + 1 if t % 2 else t - 1)) for f, t in cells]

    def swap(x):
        return lax.ppermute(x, BOTH, partner)

    def cross(x):
        return lax.ppermute(x, BOTH, pair)

    def forward(x):
        return lax.ppermute(x, BOTH, onward)

    def at(source, i):
        return source * ROWS + i * CR

    lists = (neigh_list, neigh_count, cross_list)
    whole, *chunks = norm(tokens, norm_gain[None], modulation)
    s0, s1 = swap(chunks[0]), swap(chunks[1])
    across = cross(whole)
    later, (queries, *own), (wk, wv) = own_project(whole, [w_query, w_key, w_value], [chunks[2]])
    s2 = swap(later[0])
    o0 = forward(s0)
    *held, token = kv_project([s0, across], [at(1, 0), 2 * ROWS], wk, wv, own, True)
    s1 = gate(s1, token)
    o1 = forward(s1)
    *held, token = kv_project([s1], [at(1, 1)], wk, wv, held, False)
    s2 = gate(s2, token)
    o2 = forward(s2)
    *held, att, peak, total = attend([s2, o0], [at(1, 2), at(3, 0)], wk, wv, held, queries, lists)
    parts = att, peak, total
    *held, first = attend([o1], [at(3, 1)], wk, wv, held, queries, lists, 0, parts, w_out)
    return attend([o2], [at(3, 2)], wk, wv, held, queries, lists, 1, parts, w_out, first)[2]


def solution(mesh):
    return jax.shard_map(
        local,
        mesh=mesh,
        in_specs=(
            P("frame", "tile", None),
            P(),
            P("frame", None),
            P(),
            P(),
            P(),
            P(),
            P("tile", None, None),
            P("tile", None),
            P("frame", "tile", None, None),
        ),
        out_specs=P("frame", "tile", None),
        check_vma=False,
    )
```
